512 devices in a mesh: graph: 32 (over z, core), feat: 16 (over y, x).
Axes of the slice: x: 4, y: 4, z: 16, core: 2. Of those that a mesh axis runs over, the one named last changes fastest.
Arguments:
- source_feats: bfloat16 [1024, 32768], P('feat', 'graph'), may hold values from -6 to 6
- vertex_feats: bfloat16 [1024, 1024], P('feat', 'graph'), may hold values from -6 to 6
- block_values: bfloat16 [2048, 128, 128], P('graph'), as said below
- block_target: int32 [2048], P('graph'), may hold values from 0 to 7, as said below
- block_source: int32 [2048], P('graph'), may hold values from 0 to 7
- block_count: int32 [32], P('graph'), may hold values from 1 to 64, as said below
- seed_rows: int32 [1024], P(('graph', 'feat')), may hold values from 0 to 31, as said below
- seed_weights: bfloat16 [1024, 32], P(('graph', 'feat')), may hold values from -1 to 1
- neigh_one: bfloat16 [1024, 256], P('feat'), may hold values from -0.1875 to 0.1875
- self_one: bfloat16 [1024, 256], P('feat'), may hold values from -0.1875 to 0.1875
- bias_one: float32 [256], replicated, may hold values from -3 to 3
- self_two: bfloat16 [256, 256], replicated, may hold values from -0.375 to 0.375
- neigh_two: bfloat16 [256, 256], replicated, may hold values from -0.375 to 0.375
- bias_two: float32 [256], replicated, may hold values from -3 to 3
- output_grad: bfloat16 [1024, 256], P(('graph', 'feat')), may hold values from -0.1875 to 0.1875
Outputs:
- out_two: bfloat16 [1024, 256], P(('graph', 'feat'))
- grad_neigh_one: float32 [1024, 256], P('feat')
- grad_self_one: float32 [1024, 256], P('feat')
- grad_bias_one: float32 [256], replicated
- grad_self_two: float32 [256, 256], replicated
- grad_neigh_two: float32 [256, 256], replicated
- grad_bias_two: float32 [256], replicated
The draws below stay inside these ranges and needn't reach their ends.
Inputs may be any that keep to these rules, and one draw needn't show every extreme that they name: Within a partition the 64 slots name distinct (block_target, block_source) pairs. `block_count`: some partition uses all 64 slots. `seed_rows`: distinct within a partition. `block_values`: zero where a pair has no edge.
All inputs are finite; a program needn't handle non-finite values.
Results may differ from the reference program's by a relative error of at most 0.022.
Values sent between devices are 32-bit elements; how exact they have to be, the bound alone decides.
A program may use at most 64 MiB of HBM per device.

```python
import math
import jax
import jax.numpy as jnp
from jax import lax

DIN = 1024
HID = 256
SRC_DEV = 1024
H1_DEV = 32
NBLK = 64
PARTITIONS = 32
SEED_PART = 32
NSRC = 32768
N1 = 1024
N2 = 1024
BLOCKS = 2048


def block_layout(key):
    target_blocks = H1_DEV * PARTITIONS // 128
    source_blocks = SRC_DEV // 128
    key_pairs, key_shift, key_full = jax.random.split(key, 3)
    pair_keys = jax.random.split(key_pairs, PARTITIONS)
    chosen = jax.vmap(lambda single: jax.random.permutation(single, target_blocks * source_blocks)[:NBLK])(pair_keys)
    shifts = jax.random.randint(key_shift, (PARTITIONS,), 0, 4)
    counts = jnp.maximum(jnp.right_shift(jnp.full((PARTITIONS,), NBLK, jnp.int32), shifts), 1)
    busiest = jax.random.randint(key_full, (), 0, PARTITIONS)
    counts = jnp.where(jnp.arange(PARTITIONS) == busiest, NBLK, counts)
    targets = (chosen // source_blocks).reshape(-1).astype(jnp.int32)
    sources = (chosen % source_blocks).reshape(-1).astype(jnp.int32)
    return (targets, sources, counts.astype(jnp.int32))


def draw_block_target(key, part):
    shared = block_layout(key)
    return shared[0]


def draw_block_source(key, part):
    shared = block_layout(key)
    return shared[1]


def draw_block_count(key, part):
    shared = block_layout(key)
    return shared[2]


def draw_block_values(key, part):
    key = jax.random.fold_in(key, 11)
    key_edges, key_sizes = jax.random.split(key, 2)
    shape_all = (BLOCKS, 128, 128)
    present = jax.random.bernoulli(key_edges, 1.0 / 3.0, shape_all)
    expected = 0.47 * NBLK * 16384.0 / (3.0 * H1_DEV)
    magnitude = jax.random.uniform(key_sizes, shape_all, jnp.float32, 0.5, 1.5)
    return (jnp.where(present, magnitude, 0.0) / math.sqrt(expected)).astype(jnp.bfloat16)


def draw_seed_rows(key, part):
    key = jax.random.fold_in(key, 23)
    partition_keys = jax.random.split(key, PARTITIONS)
    chosen = jax.vmap(lambda single: jax.random.permutation(single, H1_DEV)[:SEED_PART])(partition_keys)
    return chosen.reshape(-1).astype(jnp.int32)


def level_of(rng, shape, cuts, low, largest):
    def one(dim, parts):
        heights = jax.random.uniform(jax.random.fold_in(jax.random.fold_in(rng, 6), dim), (parts,), jnp.float32, low / len(cuts), largest / len(cuts))
        return jnp.repeat(jnp.exp(heights), shape[dim] // parts).reshape((-1,) + (1,) * (len(shape) - dim - 1))

    factor_of = one(*cuts[0])
    for cut in cuts[1:]:
        factor_of = factor_of * one(*cut)
    return factor_of


def bell_draw(key, extent, scale, most, shards=(), kind=jnp.bfloat16):
    entries = jax.random.normal(key, extent, jnp.float32) * scale
    if len(shards) > 0:
        entries = level_of(key, extent, shards, -0.22, 0.18) * entries
    return jnp.clip(entries, min=-most, max=most).astype(kind)


def setup_inputs(seed: int = 0) -> dict:
    key_list = jax.random.split(jax.random.key(seed), 16)
    source_feats = bell_draw(key_list[0], (DIN, NSRC), 1.0, 6.0, ((0, 16), (1, 32)))
    vertex_feats = bell_draw(key_list[1], (DIN, N1), 1.0, 6.0, ((0, 16), (1, 32)))
    block_values = draw_block_values(jax.random.fold_in(key_list[15], 71), 0)
    block_target = draw_block_target(jax.random.fold_in(key_list[15], 71), 0)
    block_source = draw_block_source(jax.random.fold_in(key_list[15], 71), 0)
    block_count = draw_block_count(jax.random.fold_in(key_list[15], 71), 0)
    seed_rows = draw_seed_rows(jax.random.fold_in(key_list[15], 71), 0)
    seed_weights = bell_draw(key_list[7], (N2, H1_DEV), H1_DEV ** -0.5, 1.0, ((0, 512),))
    neigh_one = bell_draw(key_list[8], (DIN, HID), DIN ** -0.5, 0.1875, ((0, 16),))
    self_one = bell_draw(key_list[9], (DIN, HID), DIN ** -0.5, 0.1875, ((0, 16),))
    bias_one = bell_draw(key_list[10], (HID,), 0.5, 3.0, (), jnp.float32)
    self_two = bell_draw(key_list[11], (HID, HID), HID ** -0.5, 0.375)
    neigh_two = bell_draw(key_list[12], (HID, HID), HID ** -0.5, 0.375)
    bias_two = bell_draw(key_list[13], (HID,), 0.5, 3.0, (), jnp.float32)
    output_grad = bell_draw(key_list[14], (N2, HID), 0.03, 0.1875, ((0, 512),))
    return dict(source_feats=source_feats, vertex_feats=vertex_feats, block_values=block_values, block_target=block_target, block_source=block_source, block_count=block_count, seed_rows=seed_rows, seed_weights=seed_weights, neigh_one=neigh_one, self_one=self_one, bias_one=bias_one, self_two=self_two, neigh_two=neigh_two, bias_two=bias_two, output_grad=output_grad)


norm_eps = 1e-05

def reference(source_feats, vertex_feats, block_values, block_target, block_source, block_count, seed_rows, seed_weights, neigh_one, self_one, bias_one, self_two, neigh_two, bias_two, output_grad):
    highest = lax.Precision.HIGHEST
    width_in = source_feats.shape[0]
    hop_rows = H1_DEV * PARTITIONS

    def add_block(total, index):
        owner = index // NBLK
        slot = index % NBLK
        live = slot < block_count[owner]
        first = (owner * SRC_DEV + block_source[index] * 128).astype(jnp.int32)
        columns = lax.dynamic_slice_in_dim(source_feats, first, 128, 1)
        term = jnp.dot(columns, block_values[index].T, preferred_element_type=jnp.float32)
        target = (block_target[index] * 128).astype(jnp.int32)
        current = lax.dynamic_slice_in_dim(total, target, 128, 1)
        updated = current + jnp.where(live, term, jnp.zeros_like(term))
        return (lax.dynamic_update_slice_in_dim(total, updated, target, 1), None)
    agg_feats, unused = lax.scan(add_block, jnp.zeros((width_in, hop_rows), jnp.float32), jnp.arange(BLOCKS, dtype=jnp.int32))
    pre_act = jnp.dot(agg_feats.T, neigh_one.astype(jnp.float32), precision=highest)
    pre_act = pre_act + jnp.dot(vertex_feats.T, self_one, preferred_element_type=jnp.float32)
    pre_act = pre_act + bias_one.astype(jnp.float32)
    rect = jnp.maximum(pre_act, 0.0)
    msq = lax.optimization_barrier(jnp.mean(rect * rect, axis=-1, keepdims=True))
    inverse = lax.rsqrt(msq + norm_eps)
    hidden_one = (rect * inverse).astype(jnp.bfloat16)
    grouped = hidden_one.reshape(PARTITIONS, H1_DEV, HID)
    weights_grouped = seed_weights.reshape(PARTITIONS, SEED_PART, H1_DEV)
    rows_grouped = seed_rows.reshape(PARTITIONS, SEED_PART)
    self_vals = jnp.take_along_axis(grouped, rows_grouped[:, :, None], axis=1).reshape(N2, HID)
    agg_two = jnp.einsum('psj,pjh->psh', weights_grouped.astype(jnp.float32), grouped.astype(jnp.float32), precision=highest)
    agg_two = agg_two.astype(jnp.bfloat16).reshape(N2, HID)
    out_full = jnp.dot(self_vals, self_two, preferred_element_type=jnp.float32) + jnp.dot(agg_two, neigh_two, preferred_element_type=jnp.float32)
    out_two = (out_full + bias_two.astype(jnp.float32)).astype(jnp.bfloat16)
    grad_self_two = jnp.dot(self_vals.T, output_grad, preferred_element_type=jnp.float32)
    grad_neigh_two = jnp.dot(agg_two.T, output_grad, preferred_element_type=jnp.float32)
    grad_bias_two = lax.optimization_barrier(jnp.sum(output_grad.astype(jnp.float32), axis=0))
    d_self = jnp.dot(output_grad, self_two.T, preferred_element_type=jnp.float32)
    d_agg = jnp.dot(output_grad, neigh_two.T, preferred_element_type=jnp.float32)
    picker = (rows_grouped[:, :, None] == jnp.arange(H1_DEV, dtype=jnp.int32)[None, None, :]).astype(jnp.float32)
    d_hidden = jnp.einsum('psj,psh->pjh', picker, d_self.reshape(PARTITIONS, SEED_PART, HID), precision=highest)
    d_hidden = d_hidden + jnp.einsum('psj,psh->pjh', weights_grouped.astype(jnp.float32), d_agg.reshape(PARTITIONS, SEED_PART, HID), precision=highest)
    d_hidden = d_hidden.reshape(hop_rows, HID)
    factor = lax.optimization_barrier(jnp.mean(d_hidden * rect, axis=-1, keepdims=True)) * inverse * inverse
    d_pre = jnp.where(pre_act > 0, (d_hidden - rect * factor) * inverse, jnp.zeros_like(pre_act))
    grad_neigh_one = jnp.dot(agg_feats, d_pre, precision=highest)
    grad_self_one = jnp.dot(vertex_feats.astype(jnp.float32), d_pre, precision=highest)
    grad_bias_one = lax.optimization_barrier(jnp.sum(d_pre, axis=0))
    return (out_two, grad_neigh_one, grad_self_one, grad_bias_one, grad_self_two, grad_neigh_two, grad_bias_two)
```

```python
import jax
import jax.numpy as jnp
from jax import lax
from jax.experimental import pallas as pl
from jax.experimental.pallas import tpu as pltpu
from jax.sharding import PartitionSpec as P

MESH = pl.DeviceIdType.MESH
HIGHEST = lax.Precision.HIGHEST
norm_eps = 1e-05
f32, bf16 = jnp.float32, jnp.bfloat16

NZ, NX, NF = 16, 4, 16
FAR_FIRST = (8, 7, 9, 6, 10, 5, 11, 4, 12, 3, 13, 2, 14, 1, 15)
BLOCK_ORDER = (4, 5, 3, 6, 2, 7, 1, 0)
TILES, EXTRA = 21, 5
PAIR0, EARLY, ZSUM0, XY0, XY1, PAIR1, ZSUM1, ZSUMX, ZALL, ZALLX, FALL, PAIR2, PAIR3 = (0, 4, 5, 6, 7, 8, 9, 10, 11, 12, 13, 14, 15)
PHASES = 16


def dot(a, b, ca, cb, precision=None):
    return lax.dot_general(
        a, b, (((ca,), (cb,)), ((), ())), preferred_element_type=f32, precision=precision
    )


def main_kernel(
    target_ref,
    source_ref,
    count_ref,
    rows_ref,
    src_ref,
    val_hbm,
    vert_ref,
    sw_ref,
    neigh1_ref,
    self1_ref,
    bias1_ref,
    self2_ref,
    neigh2_ref,
    bias2_ref,
    og_ref,
    out_ref,
    fin_ref,
    gfin_ref,
    val,
    order_v,
    order_s,
    early,
    agg,
    sib,
    zin,
    xy,
    hid_scr,
    g_scr,
    share,
    sib2,
    red,
    zred,
    zredx,
    local_sem,
    ssem,
    rsem,
):
    g = lax.axis_index("graph")
    f = lax.axis_index("feat")
    z, c = g // 2, g % 2
    y, x = f // 4, f % 4
    sibling = (g + 1 - 2 * c, f)

    def z_peer(off):
        return (2 * lax.rem(z + off, NZ) + c, f)

    def f_peer(off):
        return (g, lax.rem(f + off, NF))

    def x_peer(off):
        return (g, 4 * y + lax.rem(x + off, NX))

    def y_peer(off):
        return (g, 4 * lax.rem(y + off, NX) + x)

    def send(src, dst, phase, dev):
        pltpu.make_async_remote_copy(
            src_ref=src,
            dst_ref=dst,
            send_sem=ssem.at[phase],
            recv_sem=rsem.at[phase],
            device_id=dev,
            device_id_type=MESH,
        ).start()

    def recv(ref, phase):
        pltpu.make_async_remote_copy(
            src_ref=ref,
            dst_ref=ref,
            send_sem=ssem.at[phase],
            recv_sem=rsem.at[phase],
            device_id=sibling,
            device_id_type=MESH,
        ).wait_recv()

    def sent(ref, phase):
        pltpu.make_async_remote_copy(
            src_ref=ref,
            dst_ref=ref,
            send_sem=ssem.at[phase],
            recv_sem=rsem.at[phase],
            device_id=sibling,
            device_id_type=MESH,
        ).wait_send()

    fetch = pltpu.make_async_copy(val_hbm, val, local_sem.at[0])
    fetch.start()

    barrier = pltpu.get_barrier_semaphore()
    pl.semaphore_signal(barrier, inc=1, device_id=sibling, device_id_type=MESH)
    for off in FAR_FIRST:
        pl.semaphore_signal(barrier, inc=1, device_id=z_peer(off), device_id_type=MESH)
    for off in range(1, NF):
        pl.semaphore_signal(barrier, inc=1, device_id=f_peer(off), device_id_type=MESH)

    pair = target_ref[...] * 8 + source_ref[...]
    slot = lax.broadcasted_iota(jnp.int32, (64, 64), 1)
    code = jnp.where(slot >= count_ref[0], slot + 64, slot)
    hit = pair == lax.broadcasted_iota(jnp.int32, (64, 64), 0)
    picked = jnp.where(hit, code, 0)
    order_v[...] = jnp.sum(picked.T, axis=0, keepdims=True)
    to_scalar = pltpu.make_async_copy(order_v, order_s, local_sem.at[1])
    to_scalar.start()

    hop = lax.broadcasted_iota(jnp.int32, (1, 32), 1)
    og_own = og_ref[...].astype(f32)
    sw_own = sw_ref[...].astype(f32)
    hot_own = jnp.concatenate(
        [(hop == rows_ref[0]).astype(f32), (hop == rows_ref[1]).astype(f32)], axis=0
    )
    blank = jnp.zeros((2, 64), f32)
    early_own = jnp.concatenate(
        [
            og_own[:, 0:128],
            og_own[:, 128:256],
            jnp.concatenate([sw_own, hot_own, blank], axis=1),
            jnp.zeros((2, 128), f32),
        ],
        axis=0,
    )
    early[f] = early_own

    doubled = jnp.concatenate([src_ref[...], src_ref[...]], axis=0)
    low_lanes = lax.broadcasted_iota(jnp.int32, (16, 128), 1) < 64
    to_scalar.wait()
    fetch.wait()

    def block(delta):
        d = lax.rem(z // 2 + delta, 8)
        cols = []
        for s in range(8):
            k = order_s[0, d * 8 + s]
            live = jnp.where(k < 64, 1.0, 0.0).astype(bf16)
            cols.append(val[lax.rem(k, 64)] * live)
        wide = dot(jnp.concatenate(cols, axis=1), doubled, 1, 1)
        for q in range(4):
            top, bottom = wide[32 * q : 32 * q + 16], wide[32 * q + 16 : 32 * q + 32]
            agg[q % 2, 2 * d + q // 2] = jnp.where(low_lanes, top, bottom)

    def pair_rows(group):
        return [2 * lax.rem(z // 2 + delta, 8) for delta in BLOCK_ORDER[2 * group : 2 * group + 2]]

    def pair_send(group):
        for row in pair_rows(group):
            send(agg.at[1 - c, pl.ds(row, 2)], sib.at[pl.ds(row, 2)], PAIR0 + group, sibling)

    def pair_done(group):
        recv(sib.at[pl.ds(0, 4)], PAIR0 + group)
        for delta in BLOCK_ORDER[2 * group : 2 * group + 2]:
            row = 2 * lax.rem(z // 2 + delta, 8)
            if delta:
                for h in range(2):
                    agg[c, row + h] = agg[c, row + h] + sib[row + h]
                    send(agg.at[c, row + h], zin.at[z], ZSUM0, (2 * (row + h) + c, f))
            else:
                other = row + 1 - z % 2
                agg[c, other] = agg[c, other] + sib[other]
                send(agg.at[c, other], zin.at[z], ZSUM0, (2 * other + c, f))
                zin[z] = agg[c, z] + sib[z]

    for group in range(4):
        block(BLOCK_ORDER[2 * group])
        block(BLOCK_ORDER[2 * group + 1])
        if group == 0:
            pl.semaphore_wait(barrier, 31)
        pair_send(group)
        if group == 0:
            for off in range(1, NF):
                send(early.at[f], early.at[f], EARLY, f_peer(off))
        if group:
            pair_done(group - 1)
    pair_done(3)

    recv(early.at[pl.ds(0, NF - 1)], EARLY)
    og_all = jnp.concatenate(
        [
            jnp.concatenate([early[:, 0, :], early[:, 1, :]], axis=0),
            jnp.concatenate([early[:, 2, :], early[:, 3, :]], axis=0),
        ],
        axis=1,
    )
    sw_hot = jnp.concatenate([early[:, 4, :], early[:, 5, :]], axis=0)
    sw_all, hot_all = sw_hot[:, 0:32], sw_hot[:, 32:64]
    og_16 = og_all.astype(bf16)
    d_self = dot(og_16, self2_ref[...], 1, 1)
    d_agg = dot(og_16, neigh2_ref[...], 1, 1)
    d_hidden = dot(hot_all, d_self, 0, 0, HIGHEST) + dot(sw_all, d_agg, 0, 0, HIGHEST)
    bias2_part = jnp.sum(og_all, axis=0, keepdims=True)

    own_term = dot(vert_ref[...], self1_ref[...], 0, 0)

    recv(zin.at[pl.ds(0, NZ - 1)], ZSUM0)
    packed = zin[0]
    for i in range(1, NZ):
        packed = packed + zin[i]
    agg_own = jnp.concatenate([packed[:, 0:64], packed[:, 64:128]], axis=0)
    agg_hi = agg_own.astype(bf16)
    agg_lo = (agg_own - agg_hi.astype(f32)).astype(bf16)
    halves = jnp.concatenate([agg_hi, agg_lo], axis=0)
    product = dot(halves, neigh1_ref[...], 1, 0)
    partial = product[0:32] + product[32:64] + own_term

    xy[0, 0, x] = partial[:, 0:128]
    xy[0, 1, y] = partial[:, 128:256]
    for off in (2, 1, 3):
        send(xy.at[0, 0, x], xy.at[0, 0, x], XY0, x_peer(off))
        send(xy.at[0, 1, y], xy.at[0, 1, y], XY0, y_peer(off))
    recv(xy.at[0, :, pl.ds(0, 3)], XY0)
    xy[1, 0, y] = (xy[0, 0, 0] + xy[0, 0, 1]) + (xy[0, 0, 2] + xy[0, 0, 3])
    xy[1, 1, x] = (xy[0, 1, 0] + xy[0, 1, 1]) + (xy[0, 1, 2] + xy[0, 1, 3])
    for off in (2, 1, 3):
        send(xy.at[1, 0, y], xy.at[1, 0, y], XY1, y_peer(off))
        send(xy.at[1, 1, x], xy.at[1, 1, x], XY1, x_peer(off))
    recv(xy.at[1, :, pl.ds(0, 3)], XY1)
    left = (xy[1, 0, 0] + xy[1, 0, 1]) + (xy[1, 0, 2] + xy[1, 0, 3])
    right = (xy[1, 1, 0] + xy[1, 1, 1]) + (xy[1, 1, 2] + xy[1, 1, 3])
    pre_act = jnp.concatenate([left, right], axis=1) + bias1_ref[...]

    rect = jnp.maximum(pre_act, 0.0)
    msq = jnp.mean(rect * rect, axis=-1, keepdims=True)
    inverse = lax.rsqrt(msq + norm_eps)
    hidden = (rect * inverse).astype(bf16)
    factor = jnp.mean(d_hidden * rect, axis=-1, keepdims=True) * inverse * inverse
    d_pre = jnp.where(pre_act > 0, (d_hidden - rect * factor) * inverse, 0.0)
    d_pre_16 = d_pre.astype(bf16)

    hid_scr[0] = hidden[:, 0:128]
    hid_scr[1] = hidden[:, 128:256]
    mixer = jnp.where(f < 8, hot_all, sw_all).astype(bf16)
    mixed = dot(mixer, hid_scr[lax.rem(f, 8) // 4], 1, 0).astype(bf16)
    g_scr[...] = dot(mixed, og_16, 0, 0)
    g_rows = g_scr[pl.ds(pl.multiple_of(32 * lax.rem(f, 4), 32), 32), :]

    grad_neigh = dot(agg_hi, d_pre_16, 0, 0)
    grad_self = dot(vert_ref[...], d_pre_16, 1, 0)
    bias1_part = jnp.sum(d_pre, axis=0, keepdims=True)

    for a in range(8):
        for b in range(2):
            rows, cols = slice(8 * a, 8 * a + 8), slice(128 * b, 128 * b + 128)
            share[0, 2 * a + b] = grad_neigh[rows, cols]
            share[1, 2 * a + b] = grad_self[rows, cols]
    for a in range(4):
        for b in range(2):
            rows, cols = slice(8 * a, 8 * a + 8), slice(128 * b, 128 * b + 128)
            share[a // 2, 16 + 2 * (a % 2) + b] = g_rows[rows, cols]
    bias_tile = jnp.concatenate(
        [
            bias1_part[:, 0:128],
            bias1_part[:, 128:256],
            bias2_part[:, 0:128],
            bias2_part[:, 128:256],
            jnp.zeros((4, 128), f32),
        ],
        axis=0,
    )
    share[0, 20] = bias_tile
    share[1, 20] = jnp.zeros((8, 128), f32)

    send(share.at[1 - c], sib2, PAIR1, sibling)
    recv(sib2, PAIR1)
    red[...] = share[c] + sib2[...]
    for off in FAR_FIRST:
        to = lax.rem(z + off, NZ)
        send(red.at[to], zred.at[z], ZSUM1, (2 * to + c, f))
    zred[z] = red[z]
    for e in range(EXTRA):
        owner = 3 * e

        @pl.when(z != owner)
        def _():
            send(red.at[16 + e], zredx.at[z], ZSUMX, (2 * owner + c, f))

    pad = jnp.zeros((6, 32), f32)
    sw_8 = jnp.concatenate([sw_own, pad], axis=0).astype(bf16)
    hot_8 = jnp.concatenate([hot_own, pad], axis=0).astype(bf16)
    self_vals = dot(hot_8, hidden, 1, 0).astype(bf16)
    agg_two = dot(sw_8, hidden, 1, 0).astype(bf16)
    out_full = dot(self_vals, self2_ref[...], 1, 0) + dot(agg_two, neigh2_ref[...], 1, 0)
    out_ref[...] = (out_full + bias2_ref[...]).astype(bf16)[0:2]

    recv(zred.at[pl.ds(0, NZ - 1)], ZSUM1)
    total = zred[0]
    for i in range(1, NZ):
        total = total + zred[i]
    fin_ref[c, z] = total
    for off in FAR_FIRST:
        send(fin_ref.at[c, z], fin_ref.at[c, z], ZALL, z_peer(off))

    owns_extra = jnp.logical_and(lax.rem(z, 3) == 0, z < 3 * EXTRA)
    mine = 16 + z // 3

    @pl.when(owns_extra)
    def _():
        recv(zredx.at[pl.ds(0, NZ - 1)], ZSUMX)
        zredx[z] = red[mine]
        more = zredx[0]
        for i in range(1, NZ):
            more = more + zredx[i]
        fin_ref[c, mine] = more
        for off in FAR_FIRST:
            send(fin_ref.at[c, mine], fin_ref.at[c, mine], ZALLX, z_peer(off))
        recv(fin_ref.at[c, pl.ds(0, EXTRA - 1)], ZALLX)

    @pl.when(jnp.logical_not(owns_extra))
    def _():
        recv(fin_ref.at[c, pl.ds(0, EXTRA)], ZALLX)

    for off in (10, 2, 8, 6, 14, 9, 11, 5, 7, 13, 15, 1, 3, 4, 12):
        send(fin_ref.at[c, pl.ds(16, 4)], gfin_ref.at[c, f], FALL, f_peer(off))
    for t in range(4):
        gfin_ref[c, f, t] = fin_ref[c, 16 + t]
    recv(fin_ref.at[c, pl.ds(0, NZ - 1)], ZALL)
    send(fin_ref.at[c], fin_ref.at[c], PAIR2, sibling)
    recv(gfin_ref.at[c, pl.ds(0, NF - 1)], FALL)
    send(gfin_ref.at[c], gfin_ref.at[c], PAIR3, sibling)
    recv(fin_ref.at[1 - c], PAIR2)
    recv(gfin_ref.at[1 - c], PAIR3)

    for group in range(4):
        sent(sib.at[pl.ds(0, 4)], PAIR0 + group)
    sent(early.at[pl.ds(0, NF - 1)], EARLY)
    sent(zin.at[pl.ds(0, NZ - 1)], ZSUM0)
    for phase in (XY0, XY1):
        sent(xy.at[0, :, pl.ds(0, 3)], phase)
    sent(sib2, PAIR1)
    sent(zred.at[pl.ds(0, NZ - 1)], ZSUM1)

    @pl.when(owns_extra)
    def _():
        sent(zredx.at[pl.ds(0, EXTRA - 1)], ZSUMX)
        sent(zredx.at[pl.ds(0, NZ - 1)], ZALLX)

    @pl.when(jnp.logical_not(owns_extra))
    def _():
        sent(zredx.at[pl.ds(0, EXTRA)], ZSUMX)

    sent(zred.at[pl.ds(0, NZ - 1)], ZALL)
    sent(gfin_ref.at[c, pl.ds(0, NF - 1)], FALL)
    sent(fin_ref.at[c], PAIR2)
    sent(gfin_ref.at[c], PAIR3)


def lay_out_kernel(
    fin_ref, gfin_ref, out_in_ref, out_ref, neigh1_ref, self1_ref, bias1_ref, self2_ref, neigh2_ref, bias2_ref
):
    out_ref[...] = out_in_ref[...]
    for a in range(8):
        for b in range(2):
            rows, cols = slice(8 * a, 8 * a + 8), slice(128 * b, 128 * b + 128)
            neigh1_ref[rows, cols] = fin_ref[0, 2 * a + b]
            self1_ref[rows, cols] = fin_ref[1, 2 * a + b]
    bias = fin_ref[0, 20]
    bias1_ref[...] = jnp.concatenate([bias[0:1], bias[1:2]], axis=1)
    bias2_ref[...] = jnp.concatenate([bias[2:3], bias[3:4]], axis=1)
    for i in range(NF):
        ref = self2_ref if i < 8 else neigh2_ref
        for core in range(2):
            for t in range(4):
                row = 32 * (i % 8) + 16 * core + 8 * (t // 2)
                col = 128 * (t % 2)
                ref[row : row + 8, col : col + 128] = gfin_ref[core, i, t]


def body(
    source_feats,
    vertex_feats,
    block_values,
    block_target,
    block_source,
    block_count,
    seed_rows,
    seed_weights,
    neigh_one,
    self_one,
    bias_one,
    self_two,
    neigh_two,
    bias_two,
    output_grad,
):
    vmem = pl.BlockSpec(memory_space=pltpu.VMEM)
    smem = pl.BlockSpec(memory_space=pltpu.SMEM)
    hbm = pl.BlockSpec(memory_space=pl.ANY)
    out_two, fin, gfin = pl.pallas_call(
        main_kernel,
        out_shape=(
            jax.ShapeDtypeStruct((2, 256), bf16),
            jax.ShapeDtypeStruct((2, TILES, 8, 128), f32),
            jax.ShapeDtypeStruct((2, NF, 4, 8, 128), f32),
        ),
        in_specs=[vmem, vmem, smem, smem, vmem, hbm] + [vmem] * 9,
        out_specs=(vmem, vmem, vmem),
        scratch_shapes=[
            pltpu.VMEM((64, 128, 128), bf16),
            pltpu.VMEM((1, 64), jnp.int32),
            pltpu.SMEM((1, 64), jnp.int32),
            pltpu.VMEM((NF, 8, 128), f32),
            pltpu.VMEM((2, NZ, 16, 128), f32),
            pltpu.VMEM((NZ, 16, 128), f32),
            pltpu.VMEM((NZ, 16, 128), f32),
            pltpu.VMEM((2, 2, NX, 32, 128), f32),
            pltpu.VMEM((2, 32, 128), bf16),
            pltpu.VMEM((128, 256), f32),
            pltpu.VMEM((2, TILES, 8, 128), f32),
            pltpu.VMEM((TILES, 8, 128), f32),
            pltpu.VMEM((TILES, 8, 128), f32),
            pltpu.VMEM((NZ, 8, 128), f32),
            pltpu.VMEM((NZ, 8, 128), f32),
            pltpu.SemaphoreType.DMA((2,)),
            pltpu.SemaphoreType.DMA((PHASES,)),
            pltpu.SemaphoreType.DMA((PHASES,)),
        ],
        compiler_params=pltpu.CompilerParams(
            collective_id=1, has_side_effects=True, vmem_limit_bytes=32 * 2**20
        ),
    )(
        block_target.reshape(1, 64),
        block_source.reshape(1, 64),
        block_count,
        seed_rows,
        source_feats,
        block_values,
        vertex_feats,
        seed_weights,
        neigh_one,
        self_one,
        bias_one.reshape(1, 256),
        self_two,
        neigh_two,
        bias_two.reshape(1, 256),
        output_grad,
    )
    outs = pl.pallas_call(
        lay_out_kernel,
        out_shape=(
            jax.ShapeDtypeStruct((2, 256), bf16),
            jax.ShapeDtypeStruct((64, 256), f32),
            jax.ShapeDtypeStruct((64, 256), f32),
            jax.ShapeDtypeStruct((1, 256), f32),
            jax.ShapeDtypeStruct((256, 256), f32),
            jax.ShapeDtypeStruct((256, 256), f32),
            jax.ShapeDtypeStruct((1, 256), f32),
        ),
        in_specs=[vmem] * 3,
        out_specs=(vmem,) * 7,
    )(fin, gfin, out_two)
    out_two, neigh1, self1, bias1, self2, neigh2, bias2 = outs
    return out_two, neigh1, self1, bias1.reshape(256), self2, neigh2, bias2.reshape(256)


def solution(mesh):
    in_specs = (
        P("feat", "graph"),
        P("feat", "graph"),
        P("graph", None, None),
        P("graph"),
        P("graph"),
        P("graph"),
        P(("graph", "feat")),
        P(("graph", "feat"), None),
        P("feat", None),
        P("feat", None),
        P(),
        P(),
        P(),
        P(),
        P(("graph", "feat"), None),
    )
    out_specs = (P(("graph", "feat"), None), P("feat", None), P("feat", None), P(), P(), P(), P())
    return jax.shard_map(body, mesh=mesh, in_specs=in_specs, out_specs=out_specs, check_vma=False)
```

```python
import jax
import jax.numpy as jnp
from jax import lax
from jax.experimental import pallas as pl
from jax.experimental.pallas import tpu as pltpu
from jax.sharding import PartitionSpec as P

MESH = pl.DeviceIdType.MESH
HIGHEST = lax.Precision.HIGHEST
norm_eps = 1e-05
f32, bf16 = jnp.float32, jnp.bfloat16

NZ, NX, NF = 16, 4, 16
FAR_FIRST = (8, 7, 9, 6, 10, 5, 11, 4, 12, 3, 13, 2, 14, 1, 15)
BLOCK_ORDER = (4, 5, 3, 6, 2, 7, 1, 0)
TILES, EXTRA = 21, 5
PAIR0, EARLY, ZSUM0, XY0, XY1, PAIR1, ZSUM1, ZSUMX, ZALL, ZALLX, FALL, PAIR2, PAIR3 = (0, 4, 5, 6, 7, 8, 9, 10, 11, 12, 13, 14, 15)
PHASES = 16


def dot(a, b, ca, cb, precision=None):
    return lax.dot_general(
        a, b, (((ca,), (cb,)), ((), ())), preferred_element_type=f32, precision=precision
    )


def main_kernel(
    target_hbm,
    source_hbm,
    count_hbm,
    rows_hbm,
    src_hbm,
    val_hbm,
    vert_hbm,
    neigh1_hbm,
    self1_hbm,
    bias1_hbm,
    self2_hbm,
    neigh2_hbm,
    bias2_hbm,
    sw_ref,
    og_ref,
    out_ref,
    fin_ref,
    gfin_ref,
    target_ref,
    source_ref,
    count_ref,
    rows_ref,
    src_ref,
    val,
    vert_ref,
    neigh1_ref,
    self1_ref,
    bias1_ref,
    self2_ref,
    neigh2_ref,
    bias2_ref,
    order_v,
    order_s,
    early,
    agg,
    sib,
    zin,
    xy,
    hid_scr,
    g_scr,
    share,
    sib2,
    red,
    zred,
    zredx,
    local_sem,
    ssem,
    rsem,
):
    g = lax.axis_index("graph")
    f = lax.axis_index("feat")
    z, c = g // 2, g % 2
    y, x = f // 4, f % 4
    sibling = (g + 1 - 2 * c, f)

    def z_peer(off):
        return (2 * lax.rem(z + off, NZ) + c, f)

    def f_peer(off):
        return (g, lax.rem(f + off, NF))

    def x_peer(off):
        return (g, 4 * y + lax.rem(x + off, NX))

    def y_peer(off):
        return (g, 4 * lax.rem(y + off, NX) + x)

    def send(src, dst, phase, dev):
        pltpu.make_async_remote_copy(
            src_ref=src,
            dst_ref=dst,
            send_sem=ssem.at[phase],
            recv_sem=rsem.at[phase],
            device_id=dev,
            device_id_type=MESH,
        ).start()

    def recv(ref, phase):
        pltpu.make_async_remote_copy(
            src_ref=ref,
            dst_ref=ref,
            send_sem=ssem.at[phase],
            recv_sem=rsem.at[phase],
            device_id=sibling,
            device_id_type=MESH,
        ).wait_recv()

    def sent(ref, phase):
        pltpu.make_async_remote_copy(
            src_ref=ref,
            dst_ref=ref,
            send_sem=ssem.at[phase],
            recv_sem=rsem.at[phase],
            device_id=sibling,
            device_id_type=MESH,
        ).wait_send()

    pending = []

    def drain():
        for ref, phase in pending:
            sent(ref, phase)

    fetches = []
    for src, dst in (
        (target_hbm, target_ref),
        (source_hbm, source_ref),
        (count_hbm, count_ref),
        (val_hbm, val),
        (src_hbm, src_ref),
        (rows_hbm, rows_ref),
        (vert_hbm, vert_ref),
        (self1_hbm, self1_ref),
        (neigh1_hbm, neigh1_ref),
        (self2_hbm, self2_ref),
        (neigh2_hbm, neigh2_ref),
        (bias1_hbm, bias1_ref),
        (bias2_hbm, bias2_ref),
    ):
        fetches.append(pltpu.make_async_copy(src, dst, local_sem.at[1 + len(fetches)]))
        fetches[-1].start()

    barrier = pltpu.get_barrier_semaphore()
    pl.semaphore_signal(barrier, inc=1, device_id=sibling, device_id_type=MESH)
    for off in FAR_FIRST:
        pl.semaphore_signal(barrier, inc=1, device_id=z_peer(off), device_id_type=MESH)
    for off in range(1, NF):
        pl.semaphore_signal(barrier, inc=1, device_id=f_peer(off), device_id_type=MESH)

    for i in range(3):
        fetches[i].wait()
    pair = target_ref[...] * 8 + source_ref[...]
    slot = lax.broadcasted_iota(jnp.int32, (64, 64), 1)
    code = jnp.where(slot >= count_ref[0], slot + 64, slot)
    hit = pair == lax.broadcasted_iota(jnp.int32, (64, 64), 0)
    picked = jnp.where(hit, code, 0)
    order_v[...] = jnp.sum(picked.T, axis=0, keepdims=True)
    to_scalar = pltpu.make_async_copy(order_v, order_s, local_sem.at[0])
    to_scalar.start()

    fetches[5].wait()
    hop = lax.broadcasted_iota(jnp.int32, (1, 32), 1)
    og_own = og_ref[...].astype(f32)
    sw_own = sw_ref[...].astype(f32)
    hot_own = jnp.concatenate(
        [(hop == rows_ref[0]).astype(f32), (hop == rows_ref[1]).astype(f32)], axis=0
    )
    blank = jnp.zeros((2, 64), f32)
    early_own = jnp.concatenate(
        [
            og_own[:, 0:128],
            og_own[:, 128:256],
            jnp.concatenate([sw_own, hot_own, blank], axis=1),
            jnp.zeros((2, 128), f32),
        ],
        axis=0,
    )
    early[f] = early_own

    fetches[4].wait()
    doubled = jnp.concatenate([src_ref[...], src_ref[...]], axis=0)
    low_lanes = lax.broadcasted_iota(jnp.int32, (16, 128), 1) < 64
    to_scalar.wait()
    fetches[3].wait()

    def block(delta):
        d = lax.rem(z // 2 + delta, 8)
        cols = []
        for s in range(8):
            k = order_s[0, d * 8 + s]
            live = jnp.where(k < 64, 1.0, 0.0).astype(bf16)
            cols.append(val[lax.rem(k, 64)] * live)
        wide = dot(jnp.concatenate(cols, axis=1), doubled, 1, 1)
        for q in range(4):
            top, bottom = wide[32 * q : 32 * q + 16], wide[32 * q + 16 : 32 * q + 32]
            agg[q % 2, 2 * d + q // 2] = jnp.where(low_lanes, top, bottom)

    def pair_rows(group):
        return [2 * lax.rem(z // 2 + delta, 8) for delta in BLOCK_ORDER[2 * group : 2 * group + 2]]

    def pair_send(group):
        for row in pair_rows(group):
            send(agg.at[1 - c, pl.ds(row, 2)], sib.at[pl.ds(row, 2)], PAIR0 + group, sibling)

    def pair_done(group):
        recv(sib.at[pl.ds(0, 4)], PAIR0 + group)
        for delta in BLOCK_ORDER[2 * group : 2 * group + 2]:
            row = 2 * lax.rem(z // 2 + delta, 8)
            if delta:
                for h in range(2):
                    agg[c, row + h] = agg[c, row + h] + sib[row + h]
                    send(agg.at[c, row + h], zin.at[z], ZSUM0, (2 * (row + h) + c, f))
            else:
                other = row + 1 - z % 2
                agg[c, other] = agg[c, other] + sib[other]
                send(agg.at[c, other], zin.at[z], ZSUM0, (2 * other + c, f))
                zin[z] = agg[c, z] + sib[z]

    for group in range(4):
        block(BLOCK_ORDER[2 * group])
        block(BLOCK_ORDER[2 * group + 1])
        if group == 0:
            pl.semaphore_wait(barrier, 31)
        pair_send(group)
        if group == 0:
            for off in range(1, NF):
                send(early.at[f], early.at[f], EARLY, f_peer(off))
        if group:
            pair_done(group - 1)
    pair_done(3)
    pending += [(sib.at[pl.ds(0, 4)], PAIR0 + group) for group in range(4)]
    pending += [(early.at[pl.ds(0, NF - 1)], EARLY), (zin.at[pl.ds(0, NZ - 1)], ZSUM0)]

    for i in range(6, 13):
        fetches[i].wait()
    recv(early.at[pl.ds(0, NF - 1)], EARLY)
    og_all = jnp.concatenate(
        [
            jnp.concatenate([early[:, 0, :], early[:, 1, :]], axis=0),
            jnp.concatenate([early[:, 2, :], early[:, 3, :]], axis=0),
        ],
        axis=1,
    )
    sw_hot = jnp.concatenate([early[:, 4, :], early[:, 5, :]], axis=0)
    sw_all, hot_all = sw_hot[:, 0:32], sw_hot[:, 32:64]
    og_16 = og_all.astype(bf16)
    d_self = dot(og_16, self2_ref[...], 1, 1)
    d_agg = dot(og_16, neigh2_ref[...], 1, 1)
    d_hidden = dot(hot_all, d_self, 0, 0, HIGHEST) + dot(sw_all, d_agg, 0, 0, HIGHEST)
    bias2_part = jnp.sum(og_all, axis=0, keepdims=True)

    own_term = dot(vert_ref[...], self1_ref[...], 1, 0)

    recv(zin.at[pl.ds(0, NZ - 1)], ZSUM0)
    packed = zin[0]
    for i in range(1, NZ):
        packed = packed + zin[i]
    agg_own = jnp.concatenate([packed[:, 0:64], packed[:, 64:128]], axis=0)
    agg_hi = agg_own.astype(bf16)
    agg_lo = (agg_own - agg_hi.astype(f32)).astype(bf16)
    halves = jnp.concatenate([agg_hi, agg_lo], axis=0)
    product = dot(halves, neigh1_ref[...], 1, 0)
    partial = product[0:32] + product[32:64] + own_term

    xy[0, 0, x] = partial[:, 0:128]
    xy[0, 1, y] = partial[:, 128:256]
    for off in (2, 1, 3):
        send(xy.at[0, 0, x], xy.at[0, 0, x], XY0, x_peer(off))
        send(xy.at[0, 1, y], xy.at[0, 1, y], XY0, y_peer(off))
    pending.append((xy.at[0, :, pl.ds(0, 3)], XY0))
    recv(xy.at[0, :, pl.ds(0, 3)], XY0)
    xy[1, 0, y] = (xy[0, 0, 0] + xy[0, 0, 1]) + (xy[0, 0, 2] + xy[0, 0, 3])
    xy[1, 1, x] = (xy[0, 1, 0] + xy[0, 1, 1]) + (xy[0, 1, 2] + xy[0, 1, 3])
    for off in (2, 1, 3):
        send(xy.at[1, 0, y], xy.at[1, 0, y], XY1, y_peer(off))
        send(xy.at[1, 1, x], xy.at[1, 1, x], XY1, x_peer(off))
    pending.append((xy.at[1, :, pl.ds(0, 3)], XY1))
    recv(xy.at[1, :, pl.ds(0, 3)], XY1)
    left = (xy[1, 0, 0] + xy[1, 0, 1]) + (xy[1, 0, 2] + xy[1, 0, 3])
    right = (xy[1, 1, 0] + xy[1, 1, 1]) + (xy[1, 1, 2] + xy[1, 1, 3])
    pre_act = jnp.concatenate([left, right], axis=1) + bias1_ref[...]

    rect = jnp.maximum(pre_act, 0.0)
    msq = jnp.mean(rect * rect, axis=-1, keepdims=True)
    inverse = lax.rsqrt(msq + norm_eps)
    hidden = (rect * inverse).astype(bf16)
    factor = jnp.mean(d_hidden * rect, axis=-1, keepdims=True) * inverse * inverse
    d_pre = jnp.where(pre_act > 0, (d_hidden - rect * factor) * inverse, 0.0)
    d_pre_16 = d_pre.astype(bf16)

    hid_scr[0] = hidden[:, 0:128]
    hid_scr[1] = hidden[:, 128:256]
    mixer = jnp.where(f < 8, hot_all, sw_all).astype(bf16)
    mixed = dot(mixer, hid_scr[lax.rem(f, 8) // 4], 1, 0).astype(bf16)
    g_scr[...] = dot(mixed, og_16, 0, 0)
    g_rows = g_scr[pl.ds(pl.multiple_of(32 * lax.rem(f, 4), 32), 32), :]

    grad_neigh = dot(agg_hi, d_pre_16, 0, 0)
    grad_self = dot(vert_ref[...], d_pre_16, 0, 0)
    bias1_part = jnp.sum(d_pre, axis=0, keepdims=True)

    for a in range(8):
        for b in range(2):
            rows, cols = slice(8 * a, 8 * a + 8), slice(128 * b, 128 * b + 128)
            share[0, 2 * a + b] = grad_neigh[rows, cols]
            share[1, 2 * a + b] = grad_self[rows, cols]
    for a in range(4):
        for b in range(2):
            rows, cols = slice(8 * a, 8 * a + 8), slice(128 * b, 128 * b + 128)
            share[a // 2, 16 + 2 * (a % 2) + b] = g_rows[rows, cols]
    bias_tile = jnp.concatenate(
        [
            bias1_part[:, 0:128],
            bias1_part[:, 128:256],
            bias2_part[:, 0:128],
            bias2_part[:, 128:256],
            jnp.zeros((4, 128), f32),
        ],
        axis=0,
    )
    share[0, 20] = bias_tile
    share[1, 20] = jnp.zeros((8, 128), f32)

    send(share.at[1 - c], sib2, PAIR1, sibling)
    pending.append((sib2, PAIR1))
    recv(sib2, PAIR1)
    red[...] = share[c] + sib2[...]
    for off in FAR_FIRST:
        to = lax.rem(z + off, NZ)
        send(red.at[to], zred.at[z], ZSUM1, (2 * to + c, f))
    zred[z] = red[z]
    pending.append((zred.at[pl.ds(0, NZ - 1)], ZSUM1))
    for e in range(EXTRA):
        owner = 3 * e

        @pl.when(z != owner)
        def _():
            send(red.at[16 + e], zredx.at[z], ZSUMX, (2 * owner + c, f))

    pad = jnp.zeros((6, 32), f32)
    sw_8 = jnp.concatenate([sw_own, pad], axis=0).astype(bf16)
    hot_8 = jnp.concatenate([hot_own, pad], axis=0).astype(bf16)
    self_vals = dot(hot_8, hidden, 1, 0).astype(bf16)
    agg_two = dot(sw_8, hidden, 1, 0).astype(bf16)
    out_full = dot(self_vals, self2_ref[...], 1, 0) + dot(agg_two, neigh2_ref[...], 1, 0)
    out_ref[...] = (out_full + bias2_ref[...]).astype(bf16)[0:2]

    recv(zred.at[pl.ds(0, NZ - 1)], ZSUM1)
    total = zred[0]
    for i in range(1, NZ):
        total = total + zred[i]
    fin_ref[c, z] = total
    for off in FAR_FIRST:
        send(fin_ref.at[c, z], fin_ref.at[c, z], ZALL, z_peer(off))

    owns_extra = jnp.logical_and(lax.rem(z, 3) == 0, z < 3 * EXTRA)
    mine = 16 + z // 3

    @pl.when(owns_extra)
    def _():
        recv(zredx.at[pl.ds(0, NZ - 1)], ZSUMX)
        zredx[z] = red[mine]
        more = zredx[0]
        for i in range(1, NZ):
            more = more + zredx[i]
        fin_ref[c, mine] = more
        for off in FAR_FIRST:
            send(fin_ref.at[c, mine], fin_ref.at[c, mine], ZALLX, z_peer(off))
        recv(fin_ref.at[c, pl.ds(0, EXTRA - 1)], ZALLX)
        sent(zredx.at[pl.ds(0, EXTRA - 1)], ZSUMX)
        sent(zredx.at[pl.ds(0, NZ - 1)], ZALLX)

    @pl.when(jnp.logical_not(owns_extra))
    def _():
        recv(fin_ref.at[c, pl.ds(0, EXTRA)], ZALLX)
        sent(zredx.at[pl.ds(0, EXTRA)], ZSUMX)

    for off in (10, 2, 8, 6, 14, 9, 11, 5, 7, 13, 15, 1, 3, 4, 12):
        send(fin_ref.at[c, pl.ds(16, 4)], gfin_ref.at[c, f], FALL, f_peer(off))
    for t in range(4):
        gfin_ref[c, f, t] = fin_ref[c, 16 + t]
    recv(fin_ref.at[c, pl.ds(0, NZ - 1)], ZALL)
    send(fin_ref.at[c], fin_ref.at[c], PAIR2, sibling)
    recv(gfin_ref.at[c, pl.ds(0, NF - 1)], FALL)
    send(gfin_ref.at[c], gfin_ref.at[c], PAIR3, sibling)
    recv(fin_ref.at[1 - c], PAIR2)
    recv(gfin_ref.at[1 - c], PAIR3)

    pending += [
        (zred.at[pl.ds(0, NZ - 1)], ZALL),
        (gfin_ref.at[c, pl.ds(0, NF - 1)], FALL),
        (fin_ref.at[c], PAIR2),
        (gfin_ref.at[c], PAIR3),
    ]
    drain()


def lay_out_kernel(
    fin_ref, gfin_ref, out_in_ref, out_ref, neigh1_ref, self1_ref, bias1_ref, self2_ref, neigh2_ref, bias2_ref
):
    out_ref[...] = out_in_ref[...]
    for a in range(8):
        for b in range(2):
            rows, cols = slice(8 * a, 8 * a + 8), slice(128 * b, 128 * b + 128)
            neigh1_ref[rows, cols] = fin_ref[0, 2 * a + b]
            self1_ref[rows, cols] = fin_ref[1, 2 * a + b]
    bias = fin_ref[0, 20]
    bias1_ref[...] = jnp.concatenate([bias[0:1], bias[1:2]], axis=1)
    bias2_ref[...] = jnp.concatenate([bias[2:3], bias[3:4]], axis=1)
    for i in range(NF):
        ref = self2_ref if i < 8 else neigh2_ref
        for core in range(2):
            for t in range(4):
                row = 32 * (i % 8) + 16 * core + 8 * (t // 2)
                col = 128 * (t % 2)
                ref[row : row + 8, col : col + 128] = gfin_ref[core, i, t]


def body(
    source_feats,
    vertex_feats,
    block_values,
    block_target,
    block_source,
    block_count,
    seed_rows,
    seed_weights,
    neigh_one,
    self_one,
    bias_one,
    self_two,
    neigh_two,
    bias_two,
    output_grad,
):
    vmem = pl.BlockSpec(memory_space=pltpu.VMEM)
    hbm = pl.BlockSpec(memory_space=pl.ANY)
    out_two, fin, gfin = pl.pallas_call(
        main_kernel,
        out_shape=(
            jax.ShapeDtypeStruct((2, 256), bf16),
            jax.ShapeDtypeStruct((2, TILES, 8, 128), f32),
            jax.ShapeDtypeStruct((2, NF, 4, 8, 128), f32),
        ),
        in_specs=[hbm] * 13 + [vmem] * 2,
        out_specs=(vmem, vmem, vmem),
        scratch_shapes=[
            pltpu.VMEM((1, 64), jnp.int32),
            pltpu.VMEM((1, 64), jnp.int32),
            pltpu.SMEM((1,), jnp.int32),
            pltpu.SMEM((2,), jnp.int32),
            pltpu.VMEM((64, 1024), bf16),
            pltpu.VMEM((64, 128, 128), bf16),
            pltpu.VMEM((32, 64), bf16),
            pltpu.VMEM((64, 256), bf16),
            pltpu.VMEM((64, 256), bf16),
            pltpu.VMEM((1, 256), f32),
            pltpu.VMEM((256, 256), bf16),
            pltpu.VMEM((256, 256), bf16),
            pltpu.VMEM((1, 256), f32),
            pltpu.VMEM((1, 64), jnp.int32),
            pltpu.SMEM((1, 64), jnp.int32),
            pltpu.VMEM((NF, 8, 128), f32),
            pltpu.VMEM((2, NZ, 16, 128), f32),
            pltpu.VMEM((NZ, 16, 128), f32),
            pltpu.VMEM((NZ, 16, 128), f32),
            pltpu.VMEM((2, 2, NX, 32, 128), f32),
            pltpu.VMEM((2, 32, 128), bf16),
            pltpu.VMEM((128, 256), f32),
            pltpu.VMEM((2, TILES, 8, 128), f32),
            pltpu.VMEM((TILES, 8, 128), f32),
            pltpu.VMEM((TILES, 8, 128), f32),
            pltpu.VMEM((NZ, 8, 128), f32),
            pltpu.VMEM((NZ, 8, 128), f32),
            pltpu.SemaphoreType.DMA((14,)),
            pltpu.SemaphoreType.DMA((PHASES,)),
            pltpu.SemaphoreType.DMA((PHASES,)),
        ],
        compiler_params=pltpu.CompilerParams(
            collective_id=1, has_side_effects=True, vmem_limit_bytes=60 * 2**20
        ),
    )(
        block_target.reshape(1, 64),
        block_source.reshape(1, 64),
        block_count,
        seed_rows,
        source_feats,
        block_values,
        vertex_feats.T,
        neigh_one,
        self_one,
        bias_one.reshape(1, 256),
        self_two,
        neigh_two,
        bias_two.reshape(1, 256),
        seed_weights,
        output_grad,
    )
    outs = pl.pallas_call(
        lay_out_kernel,
        out_shape=(
            jax.ShapeDtypeStruct((2, 256), bf16),
            jax.ShapeDtypeStruct((64, 256), f32),
            jax.ShapeDtypeStruct((64, 256), f32),
            jax.ShapeDtypeStruct((1, 256), f32),
            jax.ShapeDtypeStruct((256, 256), f32),
            jax.ShapeDtypeStruct((256, 256), f32),
            jax.ShapeDtypeStruct((1, 256), f32),
        ),
        in_specs=[vmem] * 3,
        out_specs=(vmem,) * 7,
        compiler_params=pltpu.CompilerParams(vmem_limit_bytes=60 * 2**20),
    )(fin, gfin, out_two)
    out_two, neigh1, self1, bias1, self2, neigh2, bias2 = outs
    return out_two, neigh1, self1, bias1.reshape(256), self2, neigh2, bias2.reshape(256)


def solution(mesh):
    in_specs = (
        P("feat", "graph"),
        P("feat", "graph"),
        P("graph", None, None),
        P("graph"),
        P("graph"),
        P("graph"),
        P(("graph", "feat")),
        P(("graph", "feat"), None),
        P("feat", None),
        P("feat", None),
        P(),
        P(),
        P(),
        P(),
        P(("graph", "feat"), None),
    )
    out_specs = (P(("graph", "feat"), None), P("feat", None), P("feat", None), P(), P(), P(), P())
    return jax.shard_map(body, mesh=mesh, in_specs=in_specs, out_specs=out_specs, check_vma=False)
```

```python
import jax
import jax.numpy as jnp
from jax import lax
from jax.experimental import pallas as pl
from jax.experimental.pallas import tpu as pltpu
from jax.sharding import PartitionSpec as P

MESH = pl.DeviceIdType.MESH
HIGHEST = lax.Precision.HIGHEST
norm_eps = 1e-05
f32, bf16 = jnp.float32, jnp.bfloat16

NZ, NX, NF = 16, 4, 16
FAR_FIRST = (8, 7, 9, 6, 10, 5, 11, 4, 12, 3, 13, 2, 14, 1, 15)
FEAT_ORDER = (10, 2, 8, 6, 14, 9, 11, 5, 7, 13, 15, 1, 3, 4, 12)
BLOCK_ORDER = (4, 5, 3, 6, 2, 7, 1, 0)
(
    PAIR0, EARLY, OGZ, OGF, OGC, NBF, NBC, XY0, XY1, OWNC, VERTC, ZSUM0, AALL, ZSUM1, BALL, ZALL, FALL, FINC, GFINC,
) = (0,) + tuple(range(4, 22))
PHASES = 22


def dot(a, b, ca, cb, precision=None):
    return lax.dot_general(
        a, b, (((ca,), (cb,)), ((), ())), preferred_element_type=f32, precision=precision
    )


def main_kernel(
    target_hbm,
    source_hbm,
    count_hbm,
    rows_hbm,
    src_hbm,
    val_hbm,
    vert_hbm,
    neigh1_hbm,
    self1_hbm,
    bias1_hbm,
    self2_hbm,
    neigh2_hbm,
    bias2_hbm,
    sw_ref,
    og_ref,
    out_ref,
    bias_ref,
    fin_ref,
    gfin_ref,
    target_ref,
    source_ref,
    count_ref,
    rows_ref,
    src_ref,
    val,
    vert_ref,
    neigh1_ref,
    self1_ref,
    bias1_ref,
    self2_ref,
    neigh2_ref,
    bias2_ref,
    order_v,
    order_s,
    early,
    ogz,
    og_flat,
    nball,
    neigh_all,
    xy,
    ownt,
    vboth,
    agg,
    sib,
    zin,
    aall,
    rtile,
    zred,
    b_in,
    local_sem,
    ssem,
    rsem,
):
    g = lax.axis_index("graph")
    f = lax.axis_index("feat")
    z, c = g // 2, g % 2
    y, x = f // 4, f % 4
    sibling = (g + 1 - 2 * c, f)
    me = 16 * c + f

    def z_peer(off):
        return (2 * lax.rem(z + off, NZ) + c, f)

    def f_peer(off):
        return (g, lax.rem(f + off, NF))

    def f_across(off):
        return (g + 1 - 2 * c, lax.rem(f + off, NF))

    def x_peer(off):
        return (g, 4 * y + lax.rem(x + off, NX))

    def y_peer(off):
        return (g, 4 * lax.rem(y + off, NX) + x)

    def copy(src, dst, phase, dev):
        return pltpu.make_async_remote_copy(
            src_ref=src,
            dst_ref=dst,
            send_sem=ssem.at[phase],
            recv_sem=rsem.at[phase],
            device_id=dev,
            device_id_type=MESH,
        )

    pending = []

    def send(src, dst, phase, dev):
        copy(src, dst, phase, dev).start()

    def recv(ref, phase):
        pending.append((ref, phase))
        copy(ref, ref, phase, sibling).wait_recv()

    fetches = []
    for src, dst in (
        (target_hbm, target_ref),
        (source_hbm, source_ref),
        (count_hbm, count_ref),
        (val_hbm, val),
        (src_hbm, src_ref),
        (rows_hbm, rows_ref),
        (vert_hbm, vert_ref),
        (self1_hbm, self1_ref),
        (neigh1_hbm, neigh1_ref),
        (self2_hbm, self2_ref),
        (neigh2_hbm, neigh2_ref),
        (bias1_hbm, bias1_ref),
        (bias2_hbm, bias2_ref),
    ):
        fetches.append(pltpu.make_async_copy(src, dst, local_sem.at[1 + len(fetches)]))
        fetches[-1].start()

    barrier = pltpu.get_barrier_semaphore()

    def greet(dev):
        pl.semaphore_signal(barrier, inc=1, device_id=dev, device_id_type=MESH)

    for off in FAR_FIRST:
        greet(z_peer(off))
    for off in FEAT_ORDER:
        greet(f_peer(off))
        greet(f_across(off))
    greet(sibling)

    for i in range(3):
        fetches[i].wait()
    pair = target_ref[...] * 8 + source_ref[...]
    slot = lax.broadcasted_iota(jnp.int32, (64, 64), 1)
    code = jnp.where(slot >= count_ref[0], slot + 64, slot)
    hit = pair == lax.broadcasted_iota(jnp.int32, (64, 64), 0)
    picked = jnp.where(hit, code, 0)
    order_v[...] = jnp.sum(picked.T, axis=0, keepdims=True)
    to_scalar = pltpu.make_async_copy(order_v, order_s, local_sem.at[0])
    to_scalar.start()

    fetches[5].wait()
    hop = lax.broadcasted_iota(jnp.int32, (1, 32), 1)
    og_own = og_ref[...].astype(f32)
    sw_own = sw_ref[...].astype(f32)
    hot_own = jnp.concatenate(
        [(hop == rows_ref[0]).astype(f32), (hop == rows_ref[1]).astype(f32)], axis=0
    )
    gap = jnp.zeros((2, 32), f32)
    mix_own = jnp.where(
        c == 0,
        jnp.concatenate([sw_own, gap, hot_own, gap], axis=1),
        jnp.concatenate([gap, sw_own, gap, hot_own], axis=1),
    )
    og_rows = jnp.concatenate([og_own[:, 0:128], og_own[:, 128:256]], axis=0)
    early[me] = jnp.concatenate([og_rows, mix_own, jnp.zeros((2, 128), f32)], axis=0)
    ogz[me, z] = og_rows

    fetches[4].wait()
    doubled = jnp.concatenate([src_ref[...], src_ref[...]], axis=0)
    low_lanes = lax.broadcasted_iota(jnp.int32, (16, 128), 1) < 64
    to_scalar.wait()
    fetches[3].wait()

    for d in range(8):
        cols = []
        for s in range(8):
            k = order_s[0, d * 8 + s]
            live = jnp.where(k < 64, 1.0, 0.0).astype(bf16)
            cols.append(val[lax.rem(k, 64)] * live)
        wide = dot(jnp.concatenate(cols, axis=1), doubled, 1, 1)
        for q in range(4):
            top, bottom = wide[32 * q : 32 * q + 16], wide[32 * q + 16 : 32 * q + 32]
            agg[q % 2, 2 * d + q // 2] = jnp.where(low_lanes, top, bottom)

    for i in range(6, 13):
        fetches[i].wait()
    own_part = dot(vert_ref[...], self1_ref[...], 1, 0)
    xy[0, 0, x] = own_part[:, 0:128]
    xy[0, 1, y] = own_part[:, 128:256]
    vboth[c] = jnp.concatenate([vert_ref[...].astype(f32), jnp.zeros((32, 64), f32)], axis=1)
    nball[me] = neigh1_ref[pl.ds(pl.multiple_of(32 * c, 32), 32), :].astype(f32)

    pl.semaphore_wait(barrier, 46)

    block_rows = [2 * lax.rem(z // 2 + delta, 8) for delta in BLOCK_ORDER]
    for group in range(4):
        for row in block_rows[2 * group : 2 * group + 2]:
            send(agg.at[1 - c, pl.ds(row, 2)], sib.at[pl.ds(row, 2)], PAIR0 + group, sibling)
    for off in (2, 1, 3):
        send(xy.at[0, 0, x], xy.at[0, 0, x], XY0, x_peer(off))
        send(xy.at[0, 1, y], xy.at[0, 1, y], XY0, y_peer(off))
    for group in range(4):
        recv(sib.at[pl.ds(0, 4)], PAIR0 + group)
        for delta in BLOCK_ORDER[2 * group : 2 * group + 2]:
            row = 2 * lax.rem(z // 2 + delta, 8)
            if delta:
                for h in range(2):
                    agg[c, row + h] = agg[c, row + h] + sib[row + h]
                    send(agg.at[c, row + h], zin.at[z], ZSUM0, (2 * (row + h) + c, f))
            else:
                other = row + 1 - z % 2
                agg[c, other] = agg[c, other] + sib[other]
                send(agg.at[c, other], zin.at[z], ZSUM0, (2 * other + c, f))
                zin[z] = agg[c, z] + sib[z]
    for off in FEAT_ORDER:
        send(nball.at[me], nball.at[me], NBF, f_peer(off))
    for off in FEAT_ORDER:
        send(early.at[me], early.at[me], EARLY, f_peer(off))
        send(early.at[me], early.at[me], EARLY, f_across(off))
    send(early.at[me], early.at[me], EARLY, sibling)
    send(vboth.at[c], vboth.at[c], VERTC, sibling)

    recv(xy.at[0, :, pl.ds(0, 3)], XY0)
    xy[1, 0, y] = (xy[0, 0, 0] + xy[0, 0, 1]) + (xy[0, 0, 2] + xy[0, 0, 3])
    xy[1, 1, x] = (xy[0, 1, 0] + xy[0, 1, 1]) + (xy[0, 1, 2] + xy[0, 1, 3])
    for off in (2, 1, 3):
        send(xy.at[1, 0, y], xy.at[1, 0, y], XY1, y_peer(off))
        send(xy.at[1, 1, x], xy.at[1, 1, x], XY1, x_peer(off))
    for off in FAR_FIRST:
        send(ogz.at[me, z], ogz.at[me, z], OGZ, z_peer(off))

    recv(zin.at[pl.ds(0, NZ - 1)], ZSUM0)
    packed = [zin[i] for i in range(NZ)]
    while len(packed) > 1:
        packed = [packed[i] + packed[i + 1] for i in range(0, len(packed), 2)]
    aall[me] = packed[0]
    for off in FEAT_ORDER:
        send(aall.at[me], aall.at[me], AALL, f_peer(off))
        send(aall.at[me], aall.at[me], AALL, f_across(off))
    send(aall.at[me], aall.at[me], AALL, sibling)

    recv(nball.at[pl.ds(0, 15)], NBF)
    send(nball.at[pl.ds(16 * c, 16)], nball.at[pl.ds(16 * c, 16)], NBC, sibling)
    recv(xy.at[1, :, pl.ds(0, 3)], XY1)
    ownt[c, :, 0:128] = (xy[1, 0, 0] + xy[1, 0, 1]) + (xy[1, 0, 2] + xy[1, 0, 3])
    ownt[c, :, 128:256] = (xy[1, 1, 0] + xy[1, 1, 1]) + (xy[1, 1, 2] + xy[1, 1, 3])
    send(ownt.at[c], ownt.at[c], OWNC, sibling)

    recv(early.at[pl.ds(0, 31)], EARLY)
    groups = [(16 * core + 8 * half, r) for core in range(2) for half in range(2) for r in range(2)]
    og_64 = jnp.concatenate(
        [
            jnp.concatenate([early[i : i + 8, r, :], early[i : i + 8, 2 + r, :]], axis=1)
            for i, r in groups
        ],
        axis=0,
    ).astype(bf16)
    mix = jnp.concatenate([early[i : i + 8, 4 + r, :] for i, r in groups], axis=0)
    weight_mix, hot_mix = mix[:, 0:64], mix[:, 64:128]
    d_self = dot(og_64, self2_ref[...], 1, 1)
    d_agg = dot(og_64, neigh2_ref[...], 1, 1)
    d_hidden = dot(hot_mix, d_self, 0, 0, HIGHEST) + dot(weight_mix, d_agg, 0, 0, HIGHEST)
    mixer = jnp.where(f < 8, hot_mix, weight_mix).astype(bf16)

    recv(nball.at[pl.ds(0, 16)], NBC)
    for i in range(NF):
        for half in range(2):
            neigh_all[64 * i + 32 * half : 64 * i + 32 * half + 32, :] = nball[16 * half + i].astype(bf16)
    recv(ownt.at[0], OWNC)
    own_term = jnp.concatenate([ownt[0], ownt[1]], axis=0) + bias1_ref[...]
    recv(vboth.at[0], VERTC)
    vert_64 = jnp.concatenate([vboth[0], vboth[1]], axis=0)[:, 0:64]
    column = lax.broadcasted_iota(jnp.int32, (256, 128), 0)
    lane = lax.broadcasted_iota(jnp.int32, (256, 128), 1)
    chooser = (column == 32 * lax.rem(f, 8) + 16 * c + lane % 16).astype(f32).astype(bf16)

    recv(aall.at[pl.ds(0, 31)], AALL)
    sides = []
    for core in range(2):
        tops, bottoms = [], []
        for i in range(0, NF, 2):
            even, odd = aall[16 * core + i], aall[16 * core + i + 1]
            tops.append(jnp.where(low_lanes, even, pltpu.roll(odd, 64, 1)))
            bottoms.append(jnp.where(low_lanes, pltpu.roll(even, 64, 1), odd))
        sides += [jnp.concatenate(tops, axis=1), jnp.concatenate(bottoms, axis=1)]
    agg_64 = jnp.concatenate(sides, axis=0)
    agg_hi = agg_64.astype(bf16)
    agg_lo = (agg_64 - agg_hi.astype(f32)).astype(bf16)
    product = dot(jnp.concatenate([agg_hi, agg_lo], axis=0), neigh_all[...], 1, 0)
    pre_act = product[0:64] + product[64:128] + own_term

    rect = jnp.maximum(pre_act, 0.0)
    msq = jnp.mean(rect * rect, axis=-1, keepdims=True)
    inverse = lax.rsqrt(msq + norm_eps)
    hidden = (rect * inverse).astype(bf16)
    factor = jnp.mean(d_hidden * rect, axis=-1, keepdims=True) * inverse * inverse
    d_pre = jnp.where(pre_act > 0, (d_hidden - rect * factor) * inverse, 0.0)

    own0, own1 = aall[f], aall[16 + f]
    agg_own = jnp.concatenate([own0[:, 0:64], own0[:, 64:128], own1[:, 0:64], own1[:, 64:128]], axis=0)
    left_side = jnp.where(c == 0, agg_own, vert_64).astype(bf16)
    grad = dot(left_side, d_pre.astype(bf16), 0, 0)
    for a in range(8):
        for b in range(2):
            rtile[2 * a + b, 0:8] = grad[8 * a : 8 * a + 8, 128 * b : 128 * b + 128]

    chosen = dot(hidden, chooser, 1, 0).astype(bf16)
    mixed = dot(mixer, chosen, 1, 0)
    lane8 = lax.broadcasted_iota(jnp.int32, (8, 128), 1) // 16
    tile = jnp.zeros((8, 128), f32)
    for q in range(8):
        tile = jnp.where(lane8 == q, mixed[8 * q : 8 * q + 8], tile)
    tile = tile.astype(bf16).astype(f32)
    for i in range(NZ):
        rtile[i, 8:16] = tile
    for off in FAR_FIRST:
        to = lax.rem(z + off, NZ)
        send(rtile.at[to], zred.at[z], ZSUM1, (2 * to + c, f))
    zred[z] = rtile[z]
    recv(ogz.at[me, pl.ds(0, NZ - 1)], OGZ)
    for off in FEAT_ORDER:
        send(ogz.at[me], ogz.at[me], OGF, f_peer(off))
    bias1_part = jnp.sum(d_pre, axis=0, keepdims=True)
    b_in[z] = jnp.concatenate([bias1_part[:, 0:128], bias1_part[:, 128:256]], axis=0)
    for off in FAR_FIRST:
        send(b_in.at[z], b_in.at[z], BALL, z_peer(off))

    mix_8 = jnp.concatenate([mix_own, jnp.zeros((6, 128), f32)], axis=0).astype(bf16)
    self_vals = dot(mix_8[:, 64:128], hidden, 1, 0).astype(bf16)
    agg_two = dot(mix_8[:, 0:64], hidden, 1, 0).astype(bf16)
    out_full = dot(self_vals, self2_ref[...], 1, 0) + dot(agg_two, neigh2_ref[...], 1, 0)
    out_ref[...] = (out_full + bias2_ref[...]).astype(bf16)[0:2]

    recv(ogz.at[pl.ds(0, NF - 1)], OGF)
    send(ogz.at[pl.ds(16 * c, 16)], ogz.at[pl.ds(16 * c, 16)], OGC, sibling)
    recv(zred.at[pl.ds(0, NZ - 1)], ZSUM1)
    parts = [zred[i, 0:8] for i in range(NZ)]
    while len(parts) > 1:
        parts = [parts[i] + parts[i + 1] for i in range(0, len(parts), 2)]
    fin_ref[c, z] = parts[0]
    for off in FAR_FIRST:
        send(fin_ref.at[c, z], fin_ref.at[c, z], ZALL, z_peer(off))

    recv(ogz.at[pl.ds(0, NF)], OGC)
    total2 = jnp.zeros((16, 256), f32)
    for q, (first, r) in enumerate(groups):
        for i in range(8):
            piece = jnp.concatenate([ogz[first + i, :, r, :], ogz[first + i, :, 2 + r, :]], axis=1)
            total2 = total2 + piece
            og_flat[128 * q + 16 * i : 128 * q + 16 * i + 16, :] = piece.astype(bf16)
    bias2_sum = jnp.sum(total2, axis=0, keepdims=True)

    columns = jnp.concatenate([zred[:, 8 + i, :] for i in range(8)], axis=0).T.astype(bf16)
    columns = jnp.concatenate([columns[16 * q : 16 * q + 16] for q in range(8)], axis=1)
    share = dot(columns, og_flat[...], 1, 0)
    for a in range(2):
        for b in range(2):
            gfin_ref[me, 2 * a + b] = share[8 * a : 8 * a + 8, 128 * b : 128 * b + 128]
    for off in FEAT_ORDER:
        send(gfin_ref.at[me], gfin_ref.at[me], FALL, f_peer(off))
    recv(b_in.at[pl.ds(0, NZ - 1)], BALL)
    bias1_sum = b_in[0]
    for i in range(1, NZ):
        bias1_sum = bias1_sum + b_in[i]
    bias_ref[...] = jnp.concatenate(
        [bias1_sum, bias2_sum[:, 0:128], bias2_sum[:, 128:256], jnp.zeros((4, 128), f32)], axis=0
    )

    recv(gfin_ref.at[pl.ds(0, NF - 1)], FALL)
    send(gfin_ref.at[pl.ds(16 * c, 16)], gfin_ref.at[pl.ds(16 * c, 16)], GFINC, sibling)
    recv(fin_ref.at[c, pl.ds(0, NZ - 1)], ZALL)
    send(fin_ref.at[c], fin_ref.at[c], FINC, sibling)
    recv(gfin_ref.at[pl.ds(0, NF)], GFINC)
    recv(fin_ref.at[1 - c], FINC)

    for ref, phase in pending:
        copy(ref, ref, phase, sibling).wait_send()


def lay_out_kernel(
    fin_ref, gfin_ref, out_in_ref, bias_ref, out_ref, neigh1_ref, self1_ref, bias1_ref, self2_ref, neigh2_ref, bias2_ref
):
    out_ref[...] = out_in_ref[...]
    for a in range(8):
        for b in range(2):
            rows, cols = slice(8 * a, 8 * a + 8), slice(128 * b, 128 * b + 128)
            neigh1_ref[rows, cols] = fin_ref[0, 2 * a + b]
            self1_ref[rows, cols] = fin_ref[1, 2 * a + b]
    bias = bias_ref[...]
    bias1_ref[...] = jnp.concatenate([bias[0:1], bias[1:2]], axis=1)
    bias2_ref[...] = jnp.concatenate([bias[2:3], bias[3:4]], axis=1)
    for i in range(NF):
        ref = self2_ref if i < 8 else neigh2_ref
        for core in range(2):
            for t in range(4):
                row = 32 * (i % 8) + 16 * core + 8 * (t // 2)
                col = 128 * (t % 2)
                ref[row : row + 8, col : col + 128] = gfin_ref[16 * core + i, t]


def body(
    source_feats,
    vertex_feats,
    block_values,
    block_target,
    block_source,
    block_count,
    seed_rows,
    seed_weights,
    neigh_one,
    self_one,
    bias_one,
    self_two,
    neigh_two,
    bias_two,
    output_grad,
):
    vmem = pl.BlockSpec(memory_space=pltpu.VMEM)
    hbm = pl.BlockSpec(memory_space=pl.ANY)
    out_two, bias, fin, gfin = pl.pallas_call(
        main_kernel,
        out_shape=(
            jax.ShapeDtypeStruct((2, 256), bf16),
            jax.ShapeDtypeStruct((8, 128), f32),
            jax.ShapeDtypeStruct((2, NZ, 8, 128), f32),
            jax.ShapeDtypeStruct((2 * NF, 4, 8, 128), f32),
        ),
        in_specs=[hbm] * 13 + [vmem] * 2,
        out_specs=(vmem,) * 4,
        scratch_shapes=[
            pltpu.VMEM((1, 64), jnp.int32),
            pltpu.VMEM((1, 64), jnp.int32),
            pltpu.SMEM((1,), jnp.int32),
            pltpu.SMEM((2,), jnp.int32),
            pltpu.VMEM((64, 1024), bf16),
            pltpu.VMEM((64, 128, 128), bf16),
            pltpu.VMEM((32, 64), bf16),
            pltpu.VMEM((64, 256), bf16),
            pltpu.VMEM((64, 256), bf16),
            pltpu.VMEM((1, 256), f32),
            pltpu.VMEM((256, 256), bf16),
            pltpu.VMEM((256, 256), bf16),
            pltpu.VMEM((1, 256), f32),
            pltpu.VMEM((1, 64), jnp.int32),
            pltpu.SMEM((1, 64), jnp.int32),
            pltpu.VMEM((2 * NF, 8, 128), f32),
            pltpu.VMEM((2 * NF, NZ, 4, 128), f32),
            pltpu.VMEM((1024, 256), bf16),
            pltpu.VMEM((2 * NF, 32, 256), f32),
            pltpu.VMEM((1024, 256), bf16),
            pltpu.VMEM((2, 2, NX, 32, 128), f32),
            pltpu.VMEM((2, 32, 256), f32),
            pltpu.VMEM((2, 32, 128), f32),
            pltpu.VMEM((2, NZ, 16, 128), f32),
            pltpu.VMEM((NZ, 16, 128), f32),
            pltpu.VMEM((NZ, 16, 128), f32),
            pltpu.VMEM((2 * NF, 16, 128), f32),
            pltpu.VMEM((NZ, 16, 128), f32),
            pltpu.VMEM((NZ, 16, 128), f32),
            pltpu.VMEM((NZ, 2, 128), f32),
            pltpu.SemaphoreType.DMA((14,)),
            pltpu.SemaphoreType.DMA((PHASES,)),
            pltpu.SemaphoreType.DMA((PHASES,)),
        ],
        compiler_params=pltpu.CompilerParams(
            collective_id=1, has_side_effects=True, vmem_limit_bytes=60 * 2**20
        ),
    )(
        block_target.reshape(1, 64),
        block_source.reshape(1, 64),
        block_count,
        seed_rows,
        source_feats,
        block_values,
        vertex_feats.T,
        neigh_one,
        self_one,
        bias_one.reshape(1, 256),
        self_two,
        neigh_two,
        bias_two.reshape(1, 256),
        seed_weights,
        output_grad,
    )
    outs = pl.pallas_call(
        lay_out_kernel,
        out_shape=(
            jax.ShapeDtypeStruct((2, 256), bf16),
            jax.ShapeDtypeStruct((64, 256), f32),
            jax.ShapeDtypeStruct((64, 256), f32),
            jax.ShapeDtypeStruct((1, 256), f32),
            jax.ShapeDtypeStruct((256, 256), f32),
            jax.ShapeDtypeStruct((256, 256), f32),
            jax.ShapeDtypeStruct((1, 256), f32),
        ),
        in_specs=[vmem] * 4,
        out_specs=(vmem,) * 7,
        compiler_params=pltpu.CompilerParams(vmem_limit_bytes=60 * 2**20),
    )(fin, gfin, out_two, bias)
    out_two, neigh1, self1, bias1, self2, neigh2, bias2 = outs
    return out_two, neigh1, self1, bias1.reshape(256), self2, neigh2, bias2.reshape(256)


def solution(mesh):
    in_specs = (
        P("feat", "graph"),
        P("feat", "graph"),
        P("graph", None, None),
        P("graph"),
        P("graph"),
        P("graph"),
        P(("graph", "feat")),
        P(("graph", "feat"), None),
        P("feat", None),
        P("feat", None),
        P(),
        P(),
        P(),
        P(),
        P(("graph", "feat"), None),
    )
    out_specs = (P(("graph", "feat"), None), P("feat", None), P("feat", None), P(), P(), P(), P())
    return jax.shard_map(body, mesh=mesh, in_specs=in_specs, out_specs=out_specs, check_vma=False)
```

```python
import jax
import jax.numpy as jnp
from jax import lax
from jax.experimental import pallas as pl
from jax.experimental.pallas import tpu as pltpu
from jax.sharding import PartitionSpec as P

MESH = pl.DeviceIdType.MESH
HIGHEST = lax.Precision.HIGHEST
norm_eps = 1e-05
f32, bf16 = jnp.float32, jnp.bfloat16

NZ, NX, NF = 16, 4, 16
FAR_FIRST = (8, 7, 9, 6, 10, 5, 11, 4, 12, 3, 13, 2, 14, 1, 15)
FEAT_ORDER = (10, 2, 8, 6, 14, 9, 11, 5, 7, 13, 15, 1, 3, 4, 12)
BLOCK_ORDER = (4, 5, 3, 6, 2, 7, 1, 0)
(
    PAIR0, EARLY, OGZ, OGF, OGC, NBF, NBC, XY0, XY1, OWNC, VERTC, ZSUM0, AALL, ZSUM1, BALL, ZALL, FINC, GFINC, FALL,
) = (0,) + tuple(range(4, 22))
PHASES = 25


def dot(a, b, ca, cb, precision=None):
    return lax.dot_general(
        a, b, (((ca,), (cb,)), ((), ())), preferred_element_type=f32, precision=precision
    )


def main_kernel(
    target_hbm,
    source_hbm,
    count_hbm,
    rows_hbm,
    src_hbm,
    val_hbm,
    vert_hbm,
    neigh1_hbm,
    self1_hbm,
    bias1_hbm,
    self2_hbm,
    neigh2_hbm,
    bias2_hbm,
    sw_ref,
    og_ref,
    out_hbm,
    bias1_out,
    bias2_out,
    fin_hbm,
    g2_hbm,
    out_ref,
    bias_ref,
    fin_ref,
    g2_ref,
    target_ref,
    source_ref,
    count_ref,
    rows_ref,
    src_ref,
    val,
    vert_ref,
    neigh1_ref,
    self1_ref,
    bias1_ref,
    self2_ref,
    neigh2_ref,
    bias2_ref,
    order_v,
    order_s,
    early,
    ogz,
    og_flat,
    nball,
    neigh_all,
    xy,
    ownt,
    vboth,
    agg,
    sib,
    zin,
    aall,
    rtile,
    zred,
    b_in,
    local_sem,
    put_sem,
    ssem,
    rsem,
):
    g = lax.axis_index("graph")
    f = lax.axis_index("feat")
    z, c = g // 2, g % 2
    y, x = f // 4, f % 4
    sibling = (g + 1 - 2 * c, f)
    me = 16 * c + f

    def z_peer(off):
        return (2 * lax.rem(z + off, NZ) + c, f)

    def f_peer(off):
        return (g, lax.rem(f + off, NF))

    def f_across(off):
        return (g + 1 - 2 * c, lax.rem(f + off, NF))

    def x_peer(off):
        return (g, 4 * y + lax.rem(x + off, NX))

    def y_peer(off):
        return (g, 4 * lax.rem(y + off, NX) + x)

    def copy(src, dst, phase, dev):
        return pltpu.make_async_remote_copy(
            src_ref=src,
            dst_ref=dst,
            send_sem=ssem.at[phase],
            recv_sem=rsem.at[phase],
            device_id=dev,
            device_id_type=MESH,
        )

    pending = []

    def send(src, dst, phase, dev):
        copy(src, dst, phase, dev).start()

    def recv(ref, phase):
        pending.append((ref, phase))
        copy(ref, ref, phase, sibling).wait_recv()

    fetches = []
    for src, dst in (
        (target_hbm, target_ref),
        (source_hbm, source_ref),
        (count_hbm, count_ref),
        (val_hbm, val),
        (src_hbm, src_ref),
        (rows_hbm, rows_ref),
        (vert_hbm, vert_ref),
        (self1_hbm, self1_ref),
        (neigh1_hbm, neigh1_ref),
        (self2_hbm, self2_ref),
        (neigh2_hbm, neigh2_ref),
        (bias1_hbm, bias1_ref),
        (bias2_hbm, bias2_ref),
    ):
        fetches.append(pltpu.make_async_copy(src, dst, local_sem.at[1 + len(fetches)]))
        fetches[-1].start()

    puts = []

    def put(src, dst):
        puts.append(pltpu.make_async_copy(src, dst, put_sem.at[len(puts)]))
        puts[-1].start()

    barrier = pltpu.get_barrier_semaphore()

    def greet(dev):
        pl.semaphore_signal(barrier, inc=1, device_id=dev, device_id_type=MESH)

    for off in FAR_FIRST:
        greet(z_peer(off))
    for off in FEAT_ORDER:
        greet(f_peer(off))
        greet(f_across(off))
    greet(sibling)

    for i in range(3):
        fetches[i].wait()
    pair = target_ref[...] * 8 + source_ref[...]
    slot = lax.broadcasted_iota(jnp.int32, (64, 64), 1)
    code = jnp.where(slot >= count_ref[0], slot + 64, slot)
    hit = pair == lax.broadcasted_iota(jnp.int32, (64, 64), 0)
    picked = jnp.where(hit, code, 0)
    order_v[...] = jnp.sum(picked.T, axis=0, keepdims=True)
    to_scalar = pltpu.make_async_copy(order_v, order_s, local_sem.at[0])
    to_scalar.start()

    fetches[5].wait()
    hop = lax.broadcasted_iota(jnp.int32, (1, 32), 1)
    og_own = og_ref[...].astype(f32)
    sw_own = sw_ref[...].astype(f32)
    hot_own = jnp.concatenate(
        [(hop == rows_ref[0]).astype(f32), (hop == rows_ref[1]).astype(f32)], axis=0
    )
    gap = jnp.zeros((2, 32), f32)
    mix_own = jnp.where(
        c == 0,
        jnp.concatenate([sw_own, gap, hot_own, gap], axis=1),
        jnp.concatenate([gap, sw_own, gap, hot_own], axis=1),
    )
    og_rows = jnp.concatenate([og_own[:, 0:128], og_own[:, 128:256]], axis=0)
    early[me] = jnp.concatenate([og_rows, mix_own, jnp.zeros((2, 128), f32)], axis=0)
    ogz[me, z] = og_rows

    fetches[4].wait()
    doubled = jnp.concatenate([src_ref[...], src_ref[...]], axis=0)
    low_lanes = lax.broadcasted_iota(jnp.int32, (16, 128), 1) < 64
    to_scalar.wait()
    fetches[3].wait()

    for d in range(8):
        cols = []
        for s in range(8):
            k = order_s[0, d * 8 + s]
            live = jnp.where(k < 64, 1.0, 0.0).astype(bf16)
            cols.append(val[lax.rem(k, 64)] * live)
        wide = dot(jnp.concatenate(cols, axis=1), doubled, 1, 1)
        for q in range(4):
            top, bottom = wide[32 * q : 32 * q + 16], wide[32 * q + 16 : 32 * q + 32]
            agg[q % 2, 2 * d + q // 2] = jnp.where(low_lanes, top, bottom)

    for i in range(6, 13):
        fetches[i].wait()
    own_part = dot(vert_ref[...], self1_ref[...], 1, 0)
    xy[0, 0, x] = own_part[:, 0:128]
    xy[0, 1, y] = own_part[:, 128:256]
    vboth[c] = jnp.concatenate([vert_ref[...].astype(f32), jnp.zeros((32, 64), f32)], axis=1)
    nball[me] = neigh1_ref[pl.ds(pl.multiple_of(32 * c, 32), 32), :].astype(f32)

    pl.semaphore_wait(barrier, 46)

    block_rows = [2 * lax.rem(z // 2 + delta, 8) for delta in BLOCK_ORDER]
    for group in range(4):
        for row in block_rows[2 * group : 2 * group + 2]:
            send(agg.at[1 - c, pl.ds(row, 2)], sib.at[pl.ds(row, 2)], PAIR0 + group, sibling)
    for off in (2, 1, 3):
        send(xy.at[0, 0, x], xy.at[0, 0, x], XY0, x_peer(off))
        send(xy.at[0, 1, y], xy.at[0, 1, y], XY0, y_peer(off))
    for group in range(4):
        recv(sib.at[pl.ds(0, 4)], PAIR0 + group)
        for delta in BLOCK_ORDER[2 * group : 2 * group + 2]:
            row = 2 * lax.rem(z // 2 + delta, 8)
            if delta:
                for h in range(2):
                    agg[c, row + h] = agg[c, row + h] + sib[row + h]
                    send(agg.at[c, row + h], zin.at[z], ZSUM0, (2 * (row + h) + c, f))
            else:
                other = row + 1 - z % 2
                agg[c, other] = agg[c, other] + sib[other]
                send(agg.at[c, other], zin.at[z], ZSUM0, (2 * other + c, f))
                zin[z] = agg[c, z] + sib[z]
    for off in FEAT_ORDER:
        send(nball.at[me], nball.at[me], NBF, f_peer(off))
    for off in FEAT_ORDER:
        send(early.at[me], early.at[me], EARLY, f_peer(off))
        send(early.at[me], early.at[me], EARLY, f_across(off))
    send(early.at[me], early.at[me], EARLY, sibling)
    send(vboth.at[c], vboth.at[c], VERTC, sibling)

    recv(xy.at[0, :, pl.ds(0, 3)], XY0)
    xy[1, 0, y] = (xy[0, 0, 0] + xy[0, 0, 1]) + (xy[0, 0, 2] + xy[0, 0, 3])
    xy[1, 1, x] = (xy[0, 1, 0] + xy[0, 1, 1]) + (xy[0, 1, 2] + xy[0, 1, 3])
    for off in (2, 1, 3):
        send(xy.at[1, 0, y], xy.at[1, 0, y], XY1, y_peer(off))
        send(xy.at[1, 1, x], xy.at[1, 1, x], XY1, x_peer(off))
    for off in FAR_FIRST:
        send(ogz.at[me, z], ogz.at[me, z], OGZ, z_peer(off))

    recv(zin.at[pl.ds(0, NZ - 1)], ZSUM0)
    packed = [zin[i] for i in range(NZ)]
    while len(packed) > 1:
        packed = [packed[i] + packed[i + 1] for i in range(0, len(packed), 2)]
    aall[me] = packed[0]
    for off in FEAT_ORDER:
        send(aall.at[me], aall.at[me], AALL, f_peer(off))
        send(aall.at[me], aall.at[me], AALL, f_across(off))
    send(aall.at[me], aall.at[me], AALL, sibling)

    recv(nball.at[pl.ds(0, 15)], NBF)
    send(nball.at[pl.ds(16 * c, 16)], nball.at[pl.ds(16 * c, 16)], NBC, sibling)
    recv(xy.at[1, :, pl.ds(0, 3)], XY1)
    ownt[c, :, 0:128] = (xy[1, 0, 0] + xy[1, 0, 1]) + (xy[1, 0, 2] + xy[1, 0, 3])
    ownt[c, :, 128:256] = (xy[1, 1, 0] + xy[1, 1, 1]) + (xy[1, 1, 2] + xy[1, 1, 3])
    send(ownt.at[c], ownt.at[c], OWNC, sibling)

    recv(early.at[pl.ds(0, 31)], EARLY)
    groups = [(16 * core + 8 * half, r) for core in range(2) for half in range(2) for r in range(2)]
    og_64 = jnp.concatenate(
        [
            jnp.concatenate([early[i : i + 8, r, :], early[i : i + 8, 2 + r, :]], axis=1)
            for i, r in groups
        ],
        axis=0,
    ).astype(bf16)
    mix = jnp.concatenate([early[i : i + 8, 4 + r, :] for i, r in groups], axis=0)
    weight_mix, hot_mix = mix[:, 0:64], mix[:, 64:128]
    d_self = dot(og_64, self2_ref[...], 1, 1)
    d_agg = dot(og_64, neigh2_ref[...], 1, 1)
    d_hidden = dot(hot_mix, d_self, 0, 0, HIGHEST) + dot(weight_mix, d_agg, 0, 0, HIGHEST)
    mixer = jnp.where(f < 8, hot_mix, weight_mix).astype(bf16)

    recv(nball.at[pl.ds(0, 16)], NBC)
    for i in range(NF):
        for half in range(2):
            neigh_all[64 * i + 32 * half : 64 * i + 32 * half + 32, :] = nball[16 * half + i].astype(bf16)
    recv(ownt.at[0], OWNC)
    own_term = jnp.concatenate([ownt[0], ownt[1]], axis=0) + bias1_ref[...]
    recv(vboth.at[0], VERTC)
    vert_64 = jnp.concatenate([vboth[0], vboth[1]], axis=0)[:, 0:64]
    column = lax.broadcasted_iota(jnp.int32, (256, 128), 0)
    lane = lax.broadcasted_iota(jnp.int32, (256, 128), 1)
    chooser = (column == 32 * lax.rem(f, 8) + 16 * c + lane % 16).astype(f32).astype(bf16)

    recv(ogz.at[me, pl.ds(0, NZ - 1)], OGZ)
    for off in FEAT_ORDER:
        send(ogz.at[me], ogz.at[me], OGF, f_peer(off))

    recv(aall.at[pl.ds(0, 31)], AALL)
    sides = []
    for core in range(2):
        tops, bottoms = [], []
        for i in range(0, NF, 2):
            even, odd = aall[16 * core + i], aall[16 * core + i + 1]
            tops.append(jnp.where(low_lanes, even, pltpu.roll(odd, 64, 1)))
            bottoms.append(jnp.where(low_lanes, pltpu.roll(even, 64, 1), odd))
        sides += [jnp.concatenate(tops, axis=1), jnp.concatenate(bottoms, axis=1)]
    agg_64 = jnp.concatenate(sides, axis=0)
    agg_hi = agg_64.astype(bf16)
    agg_lo = (agg_64 - agg_hi.astype(f32)).astype(bf16)
    product = dot(jnp.concatenate([agg_hi, agg_lo], axis=0), neigh_all[...], 1, 0)
    pre_act = product[0:64] + product[64:128] + own_term

    rect = jnp.maximum(pre_act, 0.0)
    msq = jnp.mean(rect * rect, axis=-1, keepdims=True)
    inverse = lax.rsqrt(msq + norm_eps)
    hidden = (rect * inverse).astype(bf16)
    factor = jnp.mean(d_hidden * rect, axis=-1, keepdims=True) * inverse * inverse
    d_pre = jnp.where(pre_act > 0, (d_hidden - rect * factor) * inverse, 0.0)

    own0, own1 = aall[f], aall[16 + f]
    agg_own = jnp.concatenate([own0[:, 0:64], own0[:, 64:128], own1[:, 0:64], own1[:, 64:128]], axis=0)
    left_side = jnp.where(c == 0, agg_own, vert_64).astype(bf16)
    grad = dot(left_side, d_pre.astype(bf16), 0, 0)
    for a in range(8):
        for b in range(2):
            rtile[2 * a + b, 0:8] = grad[8 * a : 8 * a + 8, 128 * b : 128 * b + 128]

    chosen = dot(hidden, chooser, 1, 0).astype(bf16)
    mixed = dot(mixer, chosen, 1, 0)
    lane8 = lax.broadcasted_iota(jnp.int32, (8, 128), 1) // 16
    tile = jnp.zeros((8, 128), f32)
    for q in range(8):
        tile = jnp.where(lane8 == q, mixed[8 * q : 8 * q + 8], tile)
    tile = tile.astype(bf16).astype(f32)
    for i in range(NZ):
        rtile[i, 8:16] = tile
    for off in FAR_FIRST:
        to = lax.rem(z + off, NZ)
        send(rtile.at[to], zred.at[z], ZSUM1, (2 * to + c, f))
    zred[z] = rtile[z]
    bias1_part = jnp.sum(d_pre, axis=0, keepdims=True)
    b_in[z] = jnp.concatenate([bias1_part[:, 0:128], bias1_part[:, 128:256]], axis=0)
    for off in FAR_FIRST:
        send(b_in.at[z], b_in.at[z], BALL, z_peer(off))

    recv(ogz.at[pl.ds(0, NF - 1)], OGF)
    send(ogz.at[pl.ds(16 * c, 16)], ogz.at[pl.ds(16 * c, 16)], OGC, sibling)

    mix_8 = jnp.concatenate([mix_own, jnp.zeros((6, 128), f32)], axis=0).astype(bf16)
    self_vals = dot(mix_8[:, 64:128], hidden, 1, 0).astype(bf16)
    agg_two = dot(mix_8[:, 0:64], hidden, 1, 0).astype(bf16)
    out_full = dot(self_vals, self2_ref[...], 1, 0) + dot(agg_two, neigh2_ref[...], 1, 0)
    out_ref[...] = (out_full + bias2_ref[...]).astype(bf16).astype(f32)[0:2]
    put(out_ref, out_hbm)

    recv(ogz.at[pl.ds(0, NF)], OGC)
    total2 = jnp.zeros((16, 256), f32)
    for q, (first, r) in enumerate(groups):
        for i in range(8):
            piece = jnp.concatenate([ogz[first + i, :, r, :], ogz[first + i, :, 2 + r, :]], axis=1)
            total2 = total2 + piece
            og_flat[128 * q + 16 * i : 128 * q + 16 * i + 16, :] = piece.astype(bf16)
    bias2_sum = jnp.sum(total2, axis=0, keepdims=True)

    recv(zred.at[pl.ds(0, NZ - 1)], ZSUM1)
    parts = [zred[i, 0:8] for i in range(NZ)]
    while len(parts) > 1:
        parts = [parts[i] + parts[i + 1] for i in range(0, len(parts), 2)]
    own_tile = fin_ref.at[
        c, pl.ds(pl.multiple_of(8 * (z // 2), 8), 8), pl.ds(pl.multiple_of(128 * lax.rem(z, 2), 128), 128)
    ]
    own_tile[...] = parts[0]
    for off in FAR_FIRST:
        send(own_tile, own_tile, ZALL, z_peer(off))

    columns = jnp.concatenate([zred[:, 8 + i, :] for i in range(8)], axis=0).T.astype(bf16)
    columns = jnp.concatenate([columns[16 * q : 16 * q + 16] for q in range(8)], axis=1)
    share = dot(columns, og_flat[...], 1, 0)
    own_rows = g2_ref.at[f // 8, lax.rem(f, 8), c]
    own_rows[...] = share
    for dy in (2, 1, 3, 0):
        for dx in (2, 1, 3, 0):
            if dy or dx:
                to = (g, 4 * lax.rem(y + dy, NX) + lax.rem(x + dx, NX))
                send(own_rows, own_rows, FALL + dy, to)
    recv(b_in.at[pl.ds(0, NZ - 1)], BALL)
    bias1_sum = b_in[0]
    for i in range(1, NZ):
        bias1_sum = bias1_sum + b_in[i]
    bias_ref[0] = jnp.concatenate([bias1_sum[0:1], bias1_sum[1:2]], axis=1)
    bias_ref[1] = bias2_sum
    put(bias_ref.at[0], bias1_out)
    put(bias_ref.at[1], bias2_out)

    for dy in (0, 1, 3, 2):
        recv(g2_ref.at[0, pl.ds(0, 4 if dy else 3), 0], FALL + dy)
        row = lax.rem(y + NX - dy, NX)
        here = (row // 2, pl.ds(4 * lax.rem(row, 2), 4), c)
        send(g2_ref.at[here], g2_ref.at[here], GFINC, sibling)
        put(g2_ref.at[here], g2_hbm.at[here])
    recv(zred.at[pl.ds(0, NZ - 1), pl.ds(0, 8)], ZALL)
    send(fin_ref.at[c], fin_ref.at[c], FINC, sibling)
    put(fin_ref.at[c], fin_hbm.at[c])
    recv(g2_ref.at[:, :, 0], GFINC)
    put(g2_ref.at[:, :, 1 - c], g2_hbm.at[:, :, 1 - c])
    recv(fin_ref.at[1 - c], FINC)
    put(fin_ref.at[1 - c], fin_hbm.at[1 - c])
    for one in puts:
        one.wait()

    for ref, phase in pending:
        copy(ref, ref, phase, sibling).wait_send()


def lay_out_kernel(
    out_in_ref, b1_in, b2_in, fin_in, g2_in, out_ref, neigh1_ref, self1_ref, bias1_ref, self2_ref, neigh2_ref, bias2_ref
):
    out_ref[...] = out_in_ref[...].astype(bf16)
    neigh1_ref[...] = fin_in[0]
    self1_ref[...] = fin_in[1]
    bias1_ref[...] = b1_in[...]
    bias2_ref[...] = b2_in[...]
    self2_ref[...] = g2_in[0]
    neigh2_ref[...] = g2_in[1]


def body(
    source_feats,
    vertex_feats,
    block_values,
    block_target,
    block_source,
    block_count,
    seed_rows,
    seed_weights,
    neigh_one,
    self_one,
    bias_one,
    self_two,
    neigh_two,
    bias_two,
    output_grad,
):
    vmem = pl.BlockSpec(memory_space=pltpu.VMEM)
    hbm = pl.BlockSpec(memory_space=pl.ANY)
    out_two, bias1, bias2, fin, g2 = pl.pallas_call(
        main_kernel,
        out_shape=(
            jax.ShapeDtypeStruct((2, 256), f32),
            jax.ShapeDtypeStruct((1, 256), f32),
            jax.ShapeDtypeStruct((1, 256), f32),
            jax.ShapeDtypeStruct((2, 64, 256), f32),
            jax.ShapeDtypeStruct((2, 8, 2, 16, 256), f32),
        ),
        in_specs=[hbm] * 13 + [vmem] * 2,
        out_specs=(hbm,) * 5,
        scratch_shapes=[
            pltpu.VMEM((2, 256), f32),
            pltpu.VMEM((2, 1, 256), f32),
            pltpu.VMEM((2, 64, 256), f32),
            pltpu.VMEM((2, 8, 2, 16, 256), f32),
            pltpu.VMEM((1, 64), jnp.int32),
            pltpu.VMEM((1, 64), jnp.int32),
            pltpu.SMEM((1,), jnp.int32),
            pltpu.SMEM((2,), jnp.int32),
            pltpu.VMEM((64, 1024), bf16),
            pltpu.VMEM((64, 128, 128), bf16),
            pltpu.VMEM((32, 64), bf16),
            pltpu.VMEM((64, 256), bf16),
            pltpu.VMEM((64, 256), bf16),
            pltpu.VMEM((1, 256), f32),
            pltpu.VMEM((256, 256), bf16),
            pltpu.VMEM((256, 256), bf16),
            pltpu.VMEM((1, 256), f32),
            pltpu.VMEM((1, 64), jnp.int32),
            pltpu.SMEM((1, 64), jnp.int32),
            pltpu.VMEM((2 * NF, 8, 128), f32),
            pltpu.VMEM((2 * NF, NZ, 4, 128), f32),
            pltpu.VMEM((1024, 256), bf16),
            pltpu.VMEM((2 * NF, 32, 256), f32),
            pltpu.VMEM((1024, 256), bf16),
            pltpu.VMEM((2, 2, NX, 32, 128), f32),
            pltpu.VMEM((2, 32, 256), f32),
            pltpu.VMEM((2, 32, 128), f32),
            pltpu.VMEM((2, NZ, 16, 128), f32),
            pltpu.VMEM((NZ, 16, 128), f32),
            pltpu.VMEM((NZ, 16, 128), f32),
            pltpu.VMEM((2 * NF, 16, 128), f32),
            pltpu.VMEM((NZ, 16, 128), f32),
            pltpu.VMEM((NZ, 16, 128), f32),
            pltpu.VMEM((NZ, 2, 128), f32),
            pltpu.SemaphoreType.DMA((14,)),
            pltpu.SemaphoreType.DMA((10,)),
            pltpu.SemaphoreType.DMA((PHASES,)),
            pltpu.SemaphoreType.DMA((PHASES,)),
        ],
        compiler_params=pltpu.CompilerParams(
            collective_id=1, has_side_effects=True, vmem_limit_bytes=60 * 2**20
        ),
    )(
        block_target.reshape(1, 64),
        block_source.reshape(1, 64),
        block_count,
        seed_rows,
        source_feats,
        block_values,
        vertex_feats.T,
        neigh_one,
        self_one,
        bias_one.reshape(1, 256),
        self_two,
        neigh_two,
        bias_two.reshape(1, 256),
        seed_weights,
        output_grad,
    )
    outs = pl.pallas_call(
        lay_out_kernel,
        out_shape=(
            jax.ShapeDtypeStruct((2, 256), bf16),
            jax.ShapeDtypeStruct((64, 256), f32),
            jax.ShapeDtypeStruct((64, 256), f32),
            jax.ShapeDtypeStruct((1, 256), f32),
            jax.ShapeDtypeStruct((256, 256), f32),
            jax.ShapeDtypeStruct((256, 256), f32),
            jax.ShapeDtypeStruct((1, 256), f32),
        ),
        in_specs=[vmem] * 5,
        out_specs=(vmem,) * 7,
        compiler_params=pltpu.CompilerParams(vmem_limit_bytes=60 * 2**20),
    )(out_two, bias1, bias2, fin, g2.reshape(2, 256, 256))
    out_two, neigh1, self1, bias1, self2, neigh2, bias2 = outs
    return out_two, neigh1, self1, bias1.reshape(256), self2, neigh2, bias2.reshape(256)


def solution(mesh):
    in_specs = (
        P("feat", "graph"),
        P("feat", "graph"),
        P("graph", None, None),
        P("graph"),
        P("graph"),
        P("graph"),
        P(("graph", "feat")),
        P(("graph", "feat"), None),
        P("feat", None),
        P("feat", None),
        P(),
        P(),
        P(),
        P(),
        P(("graph", "feat"), None),
    )
    out_specs = (P(("graph", "feat"), None), P("feat", None), P("feat", None), P(), P(), P(), P())
    return jax.shard_map(body, mesh=mesh, in_specs=in_specs, out_specs=out_specs, check_vma=False)
```

```python
import jax
import jax.numpy as jnp
from jax import lax
from jax.experimental import pallas as pl
from jax.experimental.pallas import tpu as pltpu
from jax.sharding import PartitionSpec as P

MESH = pl.DeviceIdType.MESH
HIGHEST = lax.Precision.HIGHEST
norm_eps = 1e-05
f32, bf16 = jnp.float32, jnp.bfloat16

NZ, NX, NF = 16, 4, 16
FAR_FIRST = (8, 7, 9, 6, 10, 5, 11, 4, 12, 3, 13, 2, 14, 1, 15)
FEAT_ORDER = (10, 2, 8, 6, 14, 9, 11, 5, 7, 13, 15, 1, 3, 4, 12)
BLOCK_ORDER = (4, 5, 3, 6, 2, 7, 1, 0)
(
    PAIR0, EARLY, EARLYC, OGZ, OGF, OGC, NBF, NBC, XY0, XY1, OWNC, VERTC, ZSUM0, AALL, AALLC, ZSUM1, BALL, ZALL,
    FINC, GFINC, FALL,
) = (0,) + tuple(range(4, 24))
PHASES = 27


def dot(a, b, ca, cb, precision=None):
    return lax.dot_general(
        a, b, (((ca,), (cb,)), ((), ())), preferred_element_type=f32, precision=precision
    )


def main_kernel(
    target_hbm,
    source_hbm,
    count_hbm,
    rows_hbm,
    src_hbm,
    val_hbm,
    vert_hbm,
    neigh1_hbm,
    self1_hbm,
    bias1_hbm,
    self2_hbm,
    neigh2_hbm,
    bias2_hbm,
    sw_ref,
    og_ref,
    out_hbm,
    bias1_out,
    bias2_out,
    fin_hbm,
    g2_hbm,
    out_ref,
    bias_ref,
    fin_ref,
    g2_ref,
    target_ref,
    source_ref,
    count_ref,
    rows_ref,
    src_ref,
    val,
    vert_ref,
    neigh1_ref,
    self1_ref,
    bias1_ref,
    self2_ref,
    neigh2_ref,
    bias2_ref,
    order_v,
    order_s,
    early,
    ogz,
    og_flat,
    nball,
    neigh_all,
    xy,
    ownt,
    vboth,
    agg,
    sib,
    zin,
    aall,
    rtile,
    zred,
    b_in,
    local_sem,
    put_sem,
    ssem,
    rsem,
):
    g = lax.axis_index("graph")
    f = lax.axis_index("feat")
    z, c = g // 2, g % 2
    y, x = f // 4, f % 4
    sibling = (g + 1 - 2 * c, f)
    me = 16 * c + f

    def z_peer(off):
        return (2 * lax.rem(z + off, NZ) + c, f)

    def f_peer(off):
        return (g, lax.rem(f + off, NF))

    def x_peer(off):
        return (g, 4 * y + lax.rem(x + off, NX))

    def y_peer(off):
        return (g, 4 * lax.rem(y + off, NX) + x)

    def copy(src, dst, phase, dev):
        return pltpu.make_async_remote_copy(
            src_ref=src,
            dst_ref=dst,
            send_sem=ssem.at[phase],
            recv_sem=rsem.at[phase],
            device_id=dev,
            device_id_type=MESH,
        )

    pending = []

    def send(src, dst, phase, dev):
        copy(src, dst, phase, dev).start()

    def recv(ref, phase):
        pending.append((ref, phase))
        copy(ref, ref, phase, sibling).wait_recv()

    fetches = []
    for src, dst in (
        (target_hbm, target_ref),
        (source_hbm, source_ref),
        (count_hbm, count_ref),
        (val_hbm, val),
        (src_hbm, src_ref),
        (rows_hbm, rows_ref),
        (vert_hbm, vert_ref),
        (self1_hbm, self1_ref),
        (neigh1_hbm, neigh1_ref),
        (self2_hbm, self2_ref),
        (neigh2_hbm, neigh2_ref),
        (bias1_hbm, bias1_ref),
        (bias2_hbm, bias2_ref),
    ):
        fetches.append(pltpu.make_async_copy(src, dst, local_sem.at[1 + len(fetches)]))
        fetches[-1].start()

    puts = []

    def put(src, dst):
        puts.append(pltpu.make_async_copy(src, dst, put_sem.at[len(puts)]))
        puts[-1].start()

    barrier = pltpu.get_barrier_semaphore()

    def greet(dev):
        pl.semaphore_signal(barrier, inc=1, device_id=dev, device_id_type=MESH)

    for off in FAR_FIRST:
        greet(z_peer(off))
    for off in FEAT_ORDER:
        greet(f_peer(off))
    greet(sibling)

    for i in range(3):
        fetches[i].wait()
    pair = target_ref[...] * 8 + source_ref[...]
    slot = lax.broadcasted_iota(jnp.int32, (64, 64), 1)
    code = jnp.where(slot >= count_ref[0], slot + 64, slot)
    hit = pair == lax.broadcasted_iota(jnp.int32, (64, 64), 0)
    picked = jnp.where(hit, code, 0)
    order_v[...] = jnp.sum(picked.T, axis=0, keepdims=True)
    to_scalar = pltpu.make_async_copy(order_v, order_s, local_sem.at[0])
    to_scalar.start()

    fetches[5].wait()
    hop = lax.broadcasted_iota(jnp.int32, (1, 32), 1)
    og_own = og_ref[...].astype(f32)
    sw_own = sw_ref[...].astype(f32)
    hot_own = jnp.concatenate(
        [(hop == rows_ref[0]).astype(f32), (hop == rows_ref[1]).astype(f32)], axis=0
    )
    gap = jnp.zeros((2, 32), f32)
    mix_own = jnp.where(
        c == 0,
        jnp.concatenate([sw_own, gap, hot_own, gap], axis=1),
        jnp.concatenate([gap, sw_own, gap, hot_own], axis=1),
    )
    og_rows = jnp.concatenate([og_own[:, 0:128], og_own[:, 128:256]], axis=0)
    early[me] = jnp.concatenate([og_rows, mix_own, jnp.zeros((2, 128), f32)], axis=0)
    ogz[me, z] = og_rows

    fetches[4].wait()
    doubled = jnp.concatenate([src_ref[...], src_ref[...]], axis=0)
    low_lanes = lax.broadcasted_iota(jnp.int32, (16, 128), 1) < 64
    to_scalar.wait()
    fetches[3].wait()

    for d in range(8):
        cols = []
        for s in range(8):
            k = order_s[0, d * 8 + s]
            live = jnp.where(k < 64, 1.0, 0.0).astype(bf16)
            cols.append(val[lax.rem(k, 64)] * live)
        wide = dot(jnp.concatenate(cols, axis=1), doubled, 1, 1)
        for q in range(4):
            top, bottom = wide[32 * q : 32 * q + 16], wide[32 * q + 16 : 32 * q + 32]
            agg[q % 2, 2 * d + q // 2] = jnp.where(low_lanes, top, bottom)

    for i in range(6, 13):
        fetches[i].wait()
    own_part = dot(vert_ref[...], self1_ref[...], 1, 0)
    xy[0, 0, x] = own_part[:, 0:128]
    xy[0, 1, y] = own_part[:, 128:256]
    vboth[c] = jnp.concatenate([vert_ref[...].astype(f32), jnp.zeros((32, 64), f32)], axis=1)
    nball[me] = neigh1_ref[pl.ds(pl.multiple_of(32 * c, 32), 32), :].astype(f32)

    pl.semaphore_wait(barrier, 31)

    block_rows = [2 * lax.rem(z // 2 + delta, 8) for delta in BLOCK_ORDER]
    for group in range(4):
        for row in block_rows[2 * group : 2 * group + 2]:
            send(agg.at[1 - c, pl.ds(row, 2)], sib.at[pl.ds(row, 2)], PAIR0 + group, sibling)
    for off in (2, 1, 3):
        send(xy.at[0, 0, x], xy.at[0, 0, x], XY0, x_peer(off))
        send(xy.at[0, 1, y], xy.at[0, 1, y], XY0, y_peer(off))
    for group in range(4):
        recv(sib.at[pl.ds(0, 4)], PAIR0 + group)
        for delta in BLOCK_ORDER[2 * group : 2 * group + 2]:
            row = 2 * lax.rem(z // 2 + delta, 8)
            if delta:
                for h in range(2):
                    agg[c, row + h] = agg[c, row + h] + sib[row + h]
                    send(agg.at[c, row + h], zin.at[z], ZSUM0, (2 * (row + h) + c, f))
            else:
                other = row + 1 - z % 2
                agg[c, other] = agg[c, other] + sib[other]
                send(agg.at[c, other], zin.at[z], ZSUM0, (2 * other + c, f))
                zin[z] = agg[c, z] + sib[z]
    for off in FEAT_ORDER:
        send(nball.at[me], nball.at[me], NBF, f_peer(off))
    for off in FEAT_ORDER:
        send(early.at[me], early.at[me], EARLY, f_peer(off))
    send(vboth.at[c], vboth.at[c], VERTC, sibling)

    recv(xy.at[0, :, pl.ds(0, 3)], XY0)
    xy[1, 0, y] = (xy[0, 0, 0] + xy[0, 0, 1]) + (xy[0, 0, 2] + xy[0, 0, 3])
    xy[1, 1, x] = (xy[0, 1, 0] + xy[0, 1, 1]) + (xy[0, 1, 2] + xy[0, 1, 3])
    for off in (2, 1, 3):
        send(xy.at[1, 0, y], xy.at[1, 0, y], XY1, y_peer(off))
        send(xy.at[1, 1, x], xy.at[1, 1, x], XY1, x_peer(off))
    for off in FAR_FIRST:
        send(ogz.at[me, z], ogz.at[me, z], OGZ, z_peer(off))

    recv(zin.at[pl.ds(0, NZ - 1)], ZSUM0)
    packed = [zin[i] for i in range(NZ)]
    while len(packed) > 1:
        packed = [packed[i] + packed[i + 1] for i in range(0, len(packed), 2)]
    aall[me] = packed[0]
    for off in FEAT_ORDER:
        send(aall.at[me], aall.at[me], AALL, f_peer(off))

    recv(nball.at[pl.ds(0, 15)], NBF)
    send(nball.at[pl.ds(16 * c, 16)], nball.at[pl.ds(16 * c, 16)], NBC, sibling)
    recv(xy.at[1, :, pl.ds(0, 3)], XY1)
    ownt[c, :, 0:128] = (xy[1, 0, 0] + xy[1, 0, 1]) + (xy[1, 0, 2] + xy[1, 0, 3])
    ownt[c, :, 128:256] = (xy[1, 1, 0] + xy[1, 1, 1]) + (xy[1, 1, 2] + xy[1, 1, 3])
    send(ownt.at[c], ownt.at[c], OWNC, sibling)

    recv(early.at[pl.ds(0, 15)], EARLY)
    send(early.at[pl.ds(16 * c, 16)], early.at[pl.ds(16 * c, 16)], EARLYC, sibling)
    recv(early.at[pl.ds(0, 16)], EARLYC)
    groups = [(16 * core + 8 * half, r) for core in range(2) for half in range(2) for r in range(2)]
    og_64 = jnp.concatenate(
        [
            jnp.concatenate([early[i : i + 8, r, :], early[i : i + 8, 2 + r, :]], axis=1)
            for i, r in groups
        ],
        axis=0,
    ).astype(bf16)
    mix = jnp.concatenate([early[i : i + 8, 4 + r, :] for i, r in groups], axis=0)
    weight_mix, hot_mix = mix[:, 0:64], mix[:, 64:128]
    d_self = dot(og_64, self2_ref[...], 1, 1)
    d_agg = dot(og_64, neigh2_ref[...], 1, 1)
    d_hidden = dot(hot_mix, d_self, 0, 0, HIGHEST) + dot(weight_mix, d_agg, 0, 0, HIGHEST)
    mixer = jnp.where(f < 8, hot_mix, weight_mix).astype(bf16)

    recv(nball.at[pl.ds(0, 16)], NBC)
    for i in range(NF):
        for half in range(2):
            neigh_all[64 * i + 32 * half : 64 * i + 32 * half + 32, :] = nball[16 * half + i].astype(bf16)
    recv(ownt.at[0], OWNC)
    own_term = jnp.concatenate([ownt[0], ownt[1]], axis=0) + bias1_ref[...]
    recv(vboth.at[0], VERTC)
    vert_64 = jnp.concatenate([vboth[0], vboth[1]], axis=0)[:, 0:64]
    column = lax.broadcasted_iota(jnp.int32, (256, 128), 0)
    lane = lax.broadcasted_iota(jnp.int32, (256, 128), 1)
    chooser = (column == 32 * lax.rem(f, 8) + 16 * c + lane % 16).astype(f32).astype(bf16)

    recv(ogz.at[me, pl.ds(0, NZ - 1)], OGZ)
    for off in FEAT_ORDER:
        send(ogz.at[me], ogz.at[me], OGF, f_peer(off))

    recv(aall.at[pl.ds(0, 15)], AALL)
    send(aall.at[pl.ds(16 * c, 16)], aall.at[pl.ds(16 * c, 16)], AALLC, sibling)
    recv(aall.at[pl.ds(0, 16)], AALLC)
    sides = []
    for core in range(2):
        tops, bottoms = [], []
        for i in range(0, NF, 2):
            even, odd = aall[16 * core + i], aall[16 * core + i + 1]
            tops.append(jnp.where(low_lanes, even, pltpu.roll(odd, 64, 1)))
            bottoms.append(jnp.where(low_lanes, pltpu.roll(even, 64, 1), odd))
        sides += [jnp.concatenate(tops, axis=1), jnp.concatenate(bottoms, axis=1)]
    agg_64 = jnp.concatenate(sides, axis=0)
    agg_hi = agg_64.astype(bf16)
    agg_lo = (agg_64 - agg_hi.astype(f32)).astype(bf16)
    product = dot(jnp.concatenate([agg_hi, agg_lo], axis=0), neigh_all[...], 1, 0)
    pre_act = product[0:64] + product[64:128] + own_term

    rect = jnp.maximum(pre_act, 0.0)
    msq = jnp.mean(rect * rect, axis=-1, keepdims=True)
    inverse = lax.rsqrt(msq + norm_eps)
    hidden = (rect * inverse).astype(bf16)
    factor = jnp.mean(d_hidden * rect, axis=-1, keepdims=True) * inverse * inverse
    d_pre = jnp.where(pre_act > 0, (d_hidden - rect * factor) * inverse, 0.0)

    own0, own1 = aall[f], aall[16 + f]
    agg_own = jnp.concatenate([own0[:, 0:64], own0[:, 64:128], own1[:, 0:64], own1[:, 64:128]], axis=0)
    left_side = jnp.where(c == 0, agg_own, vert_64).astype(bf16)
    grad = dot(left_side, d_pre.astype(bf16), 0, 0)
    for a in range(8):
        for b in range(2):
            rtile[2 * a + b, 0:8] = grad[8 * a : 8 * a + 8, 128 * b : 128 * b + 128]

    chosen = dot(hidden, chooser, 1, 0).astype(bf16)
    mixed = dot(mixer, chosen, 1, 0)
    lane8 = lax.broadcasted_iota(jnp.int32, (8, 128), 1) // 16
    tile = jnp.zeros((8, 128), f32)
    for q in range(8):
        tile = jnp.where(lane8 == q, mixed[8 * q : 8 * q + 8], tile)
    tile = tile.astype(bf16).astype(f32)
    for i in range(NZ):
        rtile[i, 8:16] = tile
    for off in FAR_FIRST:
        to = lax.rem(z + off, NZ)
        send(rtile.at[to], zred.at[z], ZSUM1, (2 * to + c, f))
    zred[z] = rtile[z]
    bias1_part = jnp.sum(d_pre, axis=0, keepdims=True)
    b_in[z] = jnp.concatenate([bias1_part[:, 0:128], bias1_part[:, 128:256]], axis=0)
    for off in FAR_FIRST:
        send(b_in.at[z], b_in.at[z], BALL, z_peer(off))

    recv(ogz.at[pl.ds(0, NF - 1)], OGF)
    send(ogz.at[pl.ds(16 * c, 16)], ogz.at[pl.ds(16 * c, 16)], OGC, sibling)

    mix_8 = jnp.concatenate([mix_own, jnp.zeros((6, 128), f32)], axis=0).astype(bf16)
    self_vals = dot(mix_8[:, 64:128], hidden, 1, 0).astype(bf16)
    agg_two = dot(mix_8[:, 0:64], hidden, 1, 0).astype(bf16)
    out_full = dot(self_vals, self2_ref[...], 1, 0) + dot(agg_two, neigh2_ref[...], 1, 0)
    out_ref[...] = (out_full + bias2_ref[...]).astype(bf16).astype(f32)[0:2]
    put(out_ref, out_hbm)

    recv(ogz.at[pl.ds(0, NF)], OGC)
    total2 = jnp.zeros((16, 256), f32)
    for q, (first, r) in enumerate(groups):
        for i in range(8):
            piece = jnp.concatenate([ogz[first + i, :, r, :], ogz[first + i, :, 2 + r, :]], axis=1)
            total2 = total2 + piece
            og_flat[128 * q + 16 * i : 128 * q + 16 * i + 16, :] = piece.astype(bf16)
    bias2_sum = jnp.sum(total2, axis=0, keepdims=True)

    recv(zred.at[pl.ds(0, NZ - 1)], ZSUM1)
    parts = [zred[i, 0:8] for i in range(NZ)]
    while len(parts) > 1:
        parts = [parts[i] + parts[i + 1] for i in range(0, len(parts), 2)]
    own_tile = fin_ref.at[
        c, pl.ds(pl.multiple_of(8 * (z // 2), 8), 8), pl.ds(pl.multiple_of(128 * lax.rem(z, 2), 128), 128)
    ]
    own_tile[...] = parts[0]
    for off in FAR_FIRST:
        send(own_tile, own_tile, ZALL, z_peer(off))

    columns = jnp.concatenate([zred[:, 8 + i, :] for i in range(8)], axis=0).T.astype(bf16)
    columns = jnp.concatenate([columns[16 * q : 16 * q + 16] for q in range(8)], axis=1)
    share = dot(columns, og_flat[...], 1, 0)
    own_rows = g2_ref.at[f // 8, lax.rem(f, 8), c]
    own_rows[...] = share
    for dy in (2, 1, 3, 0):
        for dx in (2, 1, 3, 0):
            if dy or dx:
                to = (g, 4 * lax.rem(y + dy, NX) + lax.rem(x + dx, NX))
                send(own_rows, own_rows, FALL + dy, to)
    recv(b_in.at[pl.ds(0, NZ - 1)], BALL)
    bias1_sum = b_in[0]
    for i in range(1, NZ):
        bias1_sum = bias1_sum + b_in[i]
    bias_ref[0] = jnp.concatenate([bias1_sum[0:1], bias1_sum[1:2]], axis=1)
    bias_ref[1] = bias2_sum
    put(bias_ref.at[0], bias1_out)
    put(bias_ref.at[1], bias2_out)

    for dy in (0, 1, 3, 2):
        recv(g2_ref.at[0, pl.ds(0, 4 if dy else 3), 0], FALL + dy)
        row = lax.rem(y + NX - dy, NX)
        here = (row // 2, pl.ds(4 * lax.rem(row, 2), 4), c)
        send(g2_ref.at[here], g2_ref.at[here], GFINC, sibling)
        put(g2_ref.at[here], g2_hbm.at[here])
    recv(zred.at[pl.ds(0, NZ - 1), pl.ds(0, 8)], ZALL)
    send(fin_ref.at[c], fin_ref.at[c], FINC, sibling)
    put(fin_ref.at[c], fin_hbm.at[c])
    recv(g2_ref.at[:, :, 0], GFINC)
    put(g2_ref.at[:, :, 1 - c], g2_hbm.at[:, :, 1 - c])
    recv(fin_ref.at[1 - c], FINC)
    put(fin_ref.at[1 - c], fin_hbm.at[1 - c])
    for one in puts:
        one.wait()

    for ref, phase in pending:
        copy(ref, ref, phase, sibling).wait_send()


def lay_out_kernel(
    out_in_ref, b1_in, b2_in, fin_in, g2_in, out_ref, neigh1_ref, self1_ref, bias1_ref, self2_ref, neigh2_ref, bias2_ref
):
    out_ref[...] = out_in_ref[...].astype(bf16)
    neigh1_ref[...] = fin_in[0]
    self1_ref[...] = fin_in[1]
    bias1_ref[...] = b1_in[...]
    bias2_ref[...] = b2_in[...]
    self2_ref[...] = g2_in[0]
    neigh2_ref[...] = g2_in[1]


def body(
    source_feats,
    vertex_feats,
    block_values,
    block_target,
    block_source,
    block_count,
    seed_rows,
    seed_weights,
    neigh_one,
    self_one,
    bias_one,
    self_two,
    neigh_two,
    bias_two,
    output_grad,
):
    vmem = pl.BlockSpec(memory_space=pltpu.VMEM)
    hbm = pl.BlockSpec(memory_space=pl.ANY)
    out_two, bias1, bias2, fin, g2 = pl.pallas_call(
        main_kernel,
        out_shape=(
            jax.ShapeDtypeStruct((2, 256), f32),
            jax.ShapeDtypeStruct((1, 256), f32),
            jax.ShapeDtypeStruct((1, 256), f32),
            jax.ShapeDtypeStruct((2, 64, 256), f32),
            jax.ShapeDtypeStruct((2, 8, 2, 16, 256), f32),
        ),
        in_specs=[hbm] * 13 + [vmem] * 2,
        out_specs=(hbm,) * 5,
        scratch_shapes=[
            pltpu.VMEM((2, 256), f32),
            pltpu.VMEM((2, 1, 256), f32),
            pltpu.VMEM((2, 64, 256), f32),
            pltpu.VMEM((2, 8, 2, 16, 256), f32),
            pltpu.VMEM((1, 64), jnp.int32),
            pltpu.VMEM((1, 64), jnp.int32),
            pltpu.SMEM((1,), jnp.int32),
            pltpu.SMEM((2,), jnp.int32),
            pltpu.VMEM((64, 1024), bf16),
            pltpu.VMEM((64, 128, 128), bf16),
            pltpu.VMEM((32, 64), bf16),
            pltpu.VMEM((64, 256), bf16),
            pltpu.VMEM((64, 256), bf16),
            pltpu.VMEM((1, 256), f32),
            pltpu.VMEM((256, 256), bf16),
            pltpu.VMEM((256, 256), bf16),
            pltpu.VMEM((1, 256), f32),
            pltpu.VMEM((1, 64), jnp.int32),
            pltpu.SMEM((1, 64), jnp.int32),
            pltpu.VMEM((2 * NF, 8, 128), f32),
            pltpu.VMEM((2 * NF, NZ, 4, 128), f32),
            pltpu.VMEM((1024, 256), bf16),
            pltpu.VMEM((2 * NF, 32, 256), f32),
            pltpu.VMEM((1024, 256), bf16),
            pltpu.VMEM((2, 2, NX, 32, 128), f32),
            pltpu.VMEM((2, 32, 256), f32),
            pltpu.VMEM((2, 32, 128), f32),
            pltpu.VMEM((2, NZ, 16, 128), f32),
            pltpu.VMEM((NZ, 16, 128), f32),
            pltpu.VMEM((NZ, 16, 128), f32),
            pltpu.VMEM((2 * NF, 16, 128), f32),
            pltpu.VMEM((NZ, 16, 128), f32),
            pltpu.VMEM((NZ, 16, 128), f32),
            pltpu.VMEM((NZ, 2, 128), f32),
            pltpu.SemaphoreType.DMA((14,)),
            pltpu.SemaphoreType.DMA((10,)),
            pltpu.SemaphoreType.DMA((PHASES,)),
            pltpu.SemaphoreType.DMA((PHASES,)),
        ],
        compiler_params=pltpu.CompilerParams(
            collective_id=1, has_side_effects=True, vmem_limit_bytes=60 * 2**20
        ),
    )(
        block_target.reshape(1, 64),
        block_source.reshape(1, 64),
        block_count,
        seed_rows,
        source_feats,
        block_values,
        vertex_feats.T,
        neigh_one,
        self_one,
        bias_one.reshape(1, 256),
        self_two,
        neigh_two,
        bias_two.reshape(1, 256),
        seed_weights,
        output_grad,
    )
    outs = pl.pallas_call(
        lay_out_kernel,
        out_shape=(
            jax.ShapeDtypeStruct((2, 256), bf16),
            jax.ShapeDtypeStruct((64, 256), f32),
            jax.ShapeDtypeStruct((64, 256), f32),
            jax.ShapeDtypeStruct((1, 256), f32),
            jax.ShapeDtypeStruct((256, 256), f32),
            jax.ShapeDtypeStruct((256, 256), f32),
            jax.ShapeDtypeStruct((1, 256), f32),
        ),
        in_specs=[vmem] * 5,
        out_specs=(vmem,) * 7,
        compiler_params=pltpu.CompilerParams(vmem_limit_bytes=60 * 2**20),
    )(out_two, bias1, bias2, fin, g2.reshape(2, 256, 256))
    out_two, neigh1, self1, bias1, self2, neigh2, bias2 = outs
    return out_two, neigh1, self1, bias1.reshape(256), self2, neigh2, bias2.reshape(256)


def solution(mesh):
    in_specs = (
        P("feat", "graph"),
        P("feat", "graph"),
        P("graph", None, None),
        P("graph"),
        P("graph"),
        P("graph"),
        P(("graph", "feat")),
        P(("graph", "feat"), None),
        P("feat", None),
        P("feat", None),
        P(),
        P(),
        P(),
        P(),
        P(("graph", "feat"), None),
    )
    out_specs = (P(("graph", "feat"), None), P("feat", None), P("feat", None), P(), P(), P(), P())
    return jax.shard_map(body, mesh=mesh, in_specs=in_specs, out_specs=out_specs, check_vma=False)
```

```python
import jax
import jax.numpy as jnp
from jax import lax
from jax.experimental import pallas as pl
from jax.experimental.pallas import tpu as pltpu
from jax.sharding import PartitionSpec as P

MESH = pl.DeviceIdType.MESH
HIGHEST = lax.Precision.HIGHEST
norm_eps = 1e-05
f32, bf16 = jnp.float32, jnp.bfloat16

NZ, NX, NF = 16, 4, 16
FAR_FIRST = (8, 7, 9, 6, 10, 5, 11, 4, 12, 3, 13, 2, 14, 1, 15)
FEAT_ORDER = (10, 2, 8, 6, 14, 9, 11, 5, 7, 13, 15, 1, 3, 4, 12)
BLOCK_ORDER = (4, 5, 3, 6, 2, 7, 1, 0)
(
    PAIR0, EARLY, EARLYC, OGZ, OGF, OGC, NBF, NBC, XY0, XY1, OWNC, VERTC, ZSUM0, AALL, AALLC, ZSUM1, BALL, ZALL,
    FINC, GFINC, FALL,
) = (0,) + tuple(range(4, 24))
PHASES = 27


def dot(a, b, ca, cb, precision=None):
    return lax.dot_general(
        a, b, (((ca,), (cb,)), ((), ())), preferred_element_type=f32, precision=precision
    )


def main_kernel(
    target_hbm,
    source_hbm,
    count_hbm,
    rows_hbm,
    src_hbm,
    val_hbm,
    vert_hbm,
    neigh1_hbm,
    self1_hbm,
    bias1_hbm,
    self2_hbm,
    neigh2_hbm,
    bias2_hbm,
    sw_ref,
    og_ref,
    out_hbm,
    bias1_out,
    bias2_out,
    fin_hbm,
    g2_hbm,
    out_ref,
    bias_ref,
    fin_ref,
    g2_ref,
    target_ref,
    source_ref,
    count_ref,
    rows_ref,
    src_ref,
    val,
    vert_ref,
    neigh1_ref,
    self1_ref,
    bias1_ref,
    self2_ref,
    neigh2_ref,
    bias2_ref,
    order_v,
    order_s,
    early,
    ogz,
    og_flat,
    nball,
    neigh_all,
    xy,
    ownt,
    vboth,
    agg,
    sib,
    zin,
    aall,
    rtile,
    zred,
    b_in,
    local_sem,
    put_sem,
    ssem,
    rsem,
):
    g = lax.axis_index("graph")
    f = lax.axis_index("feat")
    z, c = g // 2, g % 2
    y, x = f // 4, f % 4
    sibling = (g + 1 - 2 * c, f)
    me = 16 * c + f

    def z_peer(off):
        return (2 * lax.rem(z + off, NZ) + c, f)

    def f_peer(off):
        return (g, lax.rem(f + off, NF))

    def x_peer(off):
        return (g, 4 * y + lax.rem(x + off, NX))

    def y_peer(off):
        return (g, 4 * lax.rem(y + off, NX) + x)

    def copy(src, dst, phase, dev):
        return pltpu.make_async_remote_copy(
            src_ref=src,
            dst_ref=dst,
            send_sem=ssem.at[phase],
            recv_sem=rsem.at[phase],
            device_id=dev,
            device_id_type=MESH,
        )

    pending = []

    def send(src, dst, phase, dev):
        copy(src, dst, phase, dev).start()

    def recv(ref, phase):
        pending.append((ref, phase))
        copy(ref, ref, phase, sibling).wait_recv()

    fetches = []
    for src, dst in (
        (target_hbm, target_ref),
        (source_hbm, source_ref),
        (count_hbm, count_ref),
        (val_hbm, val),
        (src_hbm, src_ref),
        (rows_hbm, rows_ref),
        (vert_hbm, vert_ref),
        (self1_hbm, self1_ref),
        (neigh1_hbm, neigh1_ref),
        (self2_hbm, self2_ref),
        (neigh2_hbm, neigh2_ref),
        (bias1_hbm, bias1_ref),
        (bias2_hbm, bias2_ref),
    ):
        fetches.append(pltpu.make_async_copy(src, dst, local_sem.at[1 + len(fetches)]))
        fetches[-1].start()

    puts = []

    def put(src, dst):
        puts.append(pltpu.make_async_copy(src, dst, put_sem.at[len(puts)]))
        puts[-1].start()

    barrier = pltpu.get_barrier_semaphore()

    def greet(dev):
        pl.semaphore_signal(barrier, inc=1, device_id=dev, device_id_type=MESH)

    for off in FAR_FIRST:
        greet(z_peer(off))
    for off in FEAT_ORDER:
        greet(f_peer(off))
    greet(sibling)

    for i in range(3):
        fetches[i].wait()
    pair = target_ref[...] * 8 + source_ref[...]
    slot = lax.broadcasted_iota(jnp.int32, (64, 64), 1)
    code = jnp.where(slot >= count_ref[0], slot + 64, slot)
    hit = pair == lax.broadcasted_iota(jnp.int32, (64, 64), 0)
    picked = jnp.where(hit, code, 0)
    order_v[...] = jnp.sum(picked.T, axis=0, keepdims=True)
    to_scalar = pltpu.make_async_copy(order_v, order_s, local_sem.at[0])
    to_scalar.start()

    fetches[5].wait()
    hop = lax.broadcasted_iota(jnp.int32, (1, 32), 1)
    og_own = og_ref[...].astype(f32)
    sw_own = sw_ref[...].astype(f32)
    hot_own = jnp.concatenate(
        [(hop == rows_ref[0]).astype(f32), (hop == rows_ref[1]).astype(f32)], axis=0
    )
    gap = jnp.zeros((2, 32), f32)
    mix_own = jnp.where(
        c == 0,
        jnp.concatenate([sw_own, gap, hot_own, gap], axis=1),
        jnp.concatenate([gap, sw_own, gap, hot_own], axis=1),
    )
    og_rows = jnp.concatenate([og_own[:, 0:128], og_own[:, 128:256]], axis=0)
    early[me] = jnp.concatenate([og_rows, mix_own, jnp.zeros((2, 128), f32)], axis=0)
    ogz[me, z] = og_rows

    fetches[4].wait()
    doubled = jnp.concatenate([src_ref[...], src_ref[...]], axis=0)
    low_lanes = lax.broadcasted_iota(jnp.int32, (16, 128), 1) < 64
    to_scalar.wait()
    fetches[3].wait()

    for p, delta in enumerate(BLOCK_ORDER):
        d = lax.rem(z // 2 + delta, 8)
        cols = []
        for s in range(8):
            k = order_s[0, d * 8 + s]
            live = jnp.where(k < 64, 1.0, 0.0).astype(bf16)
            cols.append(val[lax.rem(k, 64)] * live)
        wide = dot(jnp.concatenate(cols, axis=1), doubled, 1, 1)
        for q in range(4):
            top, bottom = wide[32 * q : 32 * q + 16], wide[32 * q + 16 : 32 * q + 32]
            agg[q % 2, 2 * p + q // 2] = jnp.where(low_lanes, top, bottom)

    for i in range(6, 13):
        fetches[i].wait()
    own_part = dot(vert_ref[...], self1_ref[...], 1, 0)
    xy[0, 0, x] = own_part[:, 0:128]
    xy[0, 1, y] = own_part[:, 128:256]
    vboth[c] = jnp.concatenate([vert_ref[...].astype(f32), jnp.zeros((32, 64), f32)], axis=1)
    nball[me] = neigh1_ref[pl.ds(pl.multiple_of(32 * c, 32), 32), :].astype(f32)

    pl.semaphore_wait(barrier, 31)

    for group in range(4):
        piece = pl.ds(4 * group, 4)
        send(agg.at[1 - c, piece], sib.at[piece], PAIR0 + group, sibling)
    for off in (2, 1, 3):
        send(xy.at[0, 0, x], xy.at[0, 0, x], XY0, x_peer(off))
        send(xy.at[0, 1, y], xy.at[0, 1, y], XY0, y_peer(off))
    for group in range(4):
        recv(sib.at[pl.ds(0, 4)], PAIR0 + group)
        for p in (2 * group, 2 * group + 1):
            chip = 2 * lax.rem(z // 2 + BLOCK_ORDER[p], 8)
            if BLOCK_ORDER[p]:
                for h in range(2):
                    agg[c, 2 * p + h] = agg[c, 2 * p + h] + sib[2 * p + h]
                    send(agg.at[c, 2 * p + h], zin.at[z], ZSUM0, (2 * (chip + h) + c, f))
            else:
                h, mine = 1 - z % 2, z % 2
                agg[c, 2 * p + h] = agg[c, 2 * p + h] + sib[2 * p + h]
                send(agg.at[c, 2 * p + h], zin.at[z], ZSUM0, (2 * (chip + h) + c, f))
                zin[z] = agg[c, 2 * p + mine] + sib[2 * p + mine]
    for off in FEAT_ORDER:
        send(nball.at[me], nball.at[me], NBF, f_peer(off))
    for off in FEAT_ORDER:
        send(early.at[me], early.at[me], EARLY, f_peer(off))
    send(vboth.at[c], vboth.at[c], VERTC, sibling)

    recv(xy.at[0, :, pl.ds(0, 3)], XY0)
    xy[1, 0, y] = (xy[0, 0, 0] + xy[0, 0, 1]) + (xy[0, 0, 2] + xy[0, 0, 3])
    xy[1, 1, x] = (xy[0, 1, 0] + xy[0, 1, 1]) + (xy[0, 1, 2] + xy[0, 1, 3])
    for off in (2, 1, 3):
        send(xy.at[1, 0, y], xy.at[1, 0, y], XY1, y_peer(off))
        send(xy.at[1, 1, x], xy.at[1, 1, x], XY1, x_peer(off))
    for off in FAR_FIRST:
        send(ogz.at[me, z], ogz.at[me, z], OGZ, z_peer(off))

    recv(zin.at[pl.ds(0, NZ - 1)], ZSUM0)
    packed = [zin[i] for i in range(NZ)]
    while len(packed) > 1:
        packed = [packed[i] + packed[i + 1] for i in range(0, len(packed), 2)]
    aall[me] = packed[0]
    for off in FEAT_ORDER:
        send(aall.at[me], aall.at[me], AALL, f_peer(off))

    recv(nball.at[pl.ds(0, 15)], NBF)
    send(nball.at[pl.ds(16 * c, 16)], nball.at[pl.ds(16 * c, 16)], NBC, sibling)
    recv(xy.at[1, :, pl.ds(0, 3)], XY1)
    ownt[c, :, 0:128] = (xy[1, 0, 0] + xy[1, 0, 1]) + (xy[1, 0, 2] + xy[1, 0, 3])
    ownt[c, :, 128:256] = (xy[1, 1, 0] + xy[1, 1, 1]) + (xy[1, 1, 2] + xy[1, 1, 3])
    send(ownt.at[c], ownt.at[c], OWNC, sibling)

    recv(early.at[pl.ds(0, 15)], EARLY)
    send(early.at[pl.ds(16 * c, 16)], early.at[pl.ds(16 * c, 16)], EARLYC, sibling)
    recv(early.at[pl.ds(0, 16)], EARLYC)
    groups = [(16 * core + 8 * half, r) for core in range(2) for half in range(2) for r in range(2)]
    og_64 = jnp.concatenate(
        [
            jnp.concatenate([early[i : i + 8, r, :], early[i : i + 8, 2 + r, :]], axis=1)
            for i, r in groups
        ],
        axis=0,
    ).astype(bf16)
    mix = jnp.concatenate([early[i : i + 8, 4 + r, :] for i, r in groups], axis=0)
    weight_mix, hot_mix = mix[:, 0:64], mix[:, 64:128]
    d_self = dot(og_64, self2_ref[...], 1, 1)
    d_agg = dot(og_64, neigh2_ref[...], 1, 1)
    d_hidden = dot(hot_mix, d_self, 0, 0, HIGHEST) + dot(weight_mix, d_agg, 0, 0, HIGHEST)
    mixer = jnp.where(f < 8, hot_mix, weight_mix).astype(bf16)

    recv(nball.at[pl.ds(0, 16)], NBC)
    for i in range(NF):
        for half in range(2):
            neigh_all[64 * i + 32 * half : 64 * i + 32 * half + 32, :] = nball[16 * half + i].astype(bf16)
    recv(ownt.at[0], OWNC)
    own_term = jnp.concatenate([ownt[0], ownt[1]], axis=0) + bias1_ref[...]
    recv(vboth.at[0], VERTC)
    vert_64 = jnp.concatenate([vboth[0], vboth[1]], axis=0)[:, 0:64]
    column = lax.broadcasted_iota(jnp.int32, (256, 128), 0)
    lane = lax.broadcasted_iota(jnp.int32, (256, 128), 1)
    chooser = (column == 32 * lax.rem(f, 8) + 16 * c + lane % 16).astype(f32).astype(bf16)

    recv(ogz.at[me, pl.ds(0, NZ - 1)], OGZ)
    for off in FEAT_ORDER:
        send(ogz.at[me], ogz.at[me], OGF, f_peer(off))

    recv(aall.at[pl.ds(0, 15)], AALL)
    send(aall.at[pl.ds(16 * c, 16)], aall.at[pl.ds(16 * c, 16)], AALLC, sibling)
    recv(aall.at[pl.ds(0, 16)], AALLC)
    sides = []
    for core in range(2):
        tops, bottoms = [], []
        for i in range(0, NF, 2):
            even, odd = aall[16 * core + i], aall[16 * core + i + 1]
            tops.append(jnp.where(low_lanes, even, pltpu.roll(odd, 64, 1)))
            bottoms.append(jnp.where(low_lanes, pltpu.roll(even, 64, 1), odd))
        sides += [jnp.concatenate(tops, axis=1), jnp.concatenate(bottoms, axis=1)]
    agg_64 = jnp.concatenate(sides, axis=0)
    agg_hi = agg_64.astype(bf16)
    agg_lo = (agg_64 - agg_hi.astype(f32)).astype(bf16)
    product = dot(jnp.concatenate([agg_hi, agg_lo], axis=0), neigh_all[...], 1, 0)
    pre_act = product[0:64] + product[64:128] + own_term

    rect = jnp.maximum(pre_act, 0.0)
    msq = jnp.mean(rect * rect, axis=-1, keepdims=True)
    inverse = lax.rsqrt(msq + norm_eps)
    hidden = (rect * inverse).astype(bf16)
    factor = jnp.mean(d_hidden * rect, axis=-1, keepdims=True) * inverse * inverse
    d_pre = jnp.where(pre_act > 0, (d_hidden - rect * factor) * inverse, 0.0)

    own0, own1 = aall[f], aall[16 + f]
    agg_own = jnp.concatenate([own0[:, 0:64], own0[:, 64:128], own1[:, 0:64], own1[:, 64:128]], axis=0)
    left_side = jnp.where(c == 0, agg_own, vert_64).astype(bf16)
    grad = dot(left_side, d_pre.astype(bf16), 0, 0)
    for a in range(8):
        for b in range(2):
            rtile[2 * a + b, 0:8] = grad[8 * a : 8 * a + 8, 128 * b : 128 * b + 128]

    chosen = dot(hidden, chooser, 1, 0).astype(bf16)
    mixed = dot(mixer, chosen, 1, 0)
    lane8 = lax.broadcasted_iota(jnp.int32, (8, 128), 1) // 16
    tile = jnp.zeros((8, 128), f32)
    for q in range(8):
        tile = jnp.where(lane8 == q, mixed[8 * q : 8 * q + 8], tile)
    tile = tile.astype(bf16).astype(f32)
    for i in range(NZ):
        rtile[i, 8:16] = tile
    for off in FAR_FIRST:
        to = lax.rem(z + off, NZ)
        send(rtile.at[to], zred.at[z], ZSUM1, (2 * to + c, f))
    zred[z] = rtile[z]
    bias1_part = jnp.sum(d_pre, axis=0, keepdims=True)
    b_in[z] = jnp.concatenate([bias1_part[:, 0:128], bias1_part[:, 128:256]], axis=0)
    for off in FAR_FIRST:
        send(b_in.at[z], b_in.at[z], BALL, z_peer(off))

    recv(ogz.at[pl.ds(0, NF - 1)], OGF)
    send(ogz.at[pl.ds(16 * c, 16)], ogz.at[pl.ds(16 * c, 16)], OGC, sibling)

    mix_8 = jnp.concatenate([mix_own, jnp.zeros((6, 128), f32)], axis=0).astype(bf16)
    self_vals = dot(mix_8[:, 64:128], hidden, 1, 0).astype(bf16)
    agg_two = dot(mix_8[:, 0:64], hidden, 1, 0).astype(bf16)
    out_full = dot(self_vals, self2_ref[...], 1, 0) + dot(agg_two, neigh2_ref[...], 1, 0)
    out_ref[...] = (out_full + bias2_ref[...]).astype(bf16).astype(f32)[0:2]
    put(out_ref, out_hbm)

    recv(ogz.at[pl.ds(0, NF)], OGC)
    total2 = jnp.zeros((16, 256), f32)
    for q, (first, r) in enumerate(groups):
        for i in range(8):
            piece = jnp.concatenate([ogz[first + i, :, r, :], ogz[first + i, :, 2 + r, :]], axis=1)
            total2 = total2 + piece
            og_flat[128 * q + 16 * i : 128 * q + 16 * i + 16, :] = piece.astype(bf16)
    bias2_sum = jnp.sum(total2, axis=0, keepdims=True)

    recv(zred.at[pl.ds(0, NZ - 1)], ZSUM1)
    parts = [zred[i, 0:8] for i in range(NZ)]
    while len(parts) > 1:
        parts = [parts[i] + parts[i + 1] for i in range(0, len(parts), 2)]
    own_tile = fin_ref.at[
        c, pl.ds(pl.multiple_of(8 * (z // 2), 8), 8), pl.ds(pl.multiple_of(128 * lax.rem(z, 2), 128), 128)
    ]
    own_tile[...] = parts[0]
    for off in FAR_FIRST:
        send(own_tile, own_tile, ZALL, z_peer(off))

    columns = jnp.concatenate([zred[:, 8 + i, :] for i in range(8)], axis=0).T.astype(bf16)
    columns = jnp.concatenate([columns[16 * q : 16 * q + 16] for q in range(8)], axis=1)
    share = dot(columns, og_flat[...], 1, 0)
    own_rows = g2_ref.at[f // 8, lax.rem(f, 8), c]
    own_rows[...] = share
    for dy in (2, 1, 3, 0):
        for dx in (2, 1, 3, 0):
            if dy or dx:
                to = (g, 4 * lax.rem(y + dy, NX) + lax.rem(x + dx, NX))
                send(own_rows, own_rows, FALL + dy, to)
    recv(b_in.at[pl.ds(0, NZ - 1)], BALL)
    bias1_sum = b_in[0]
    for i in range(1, NZ):
        bias1_sum = bias1_sum + b_in[i]
    bias_ref[0] = jnp.concatenate([bias1_sum[0:1], bias1_sum[1:2]], axis=1)
    bias_ref[1] = bias2_sum
    put(bias_ref.at[0], bias1_out)
    put(bias_ref.at[1], bias2_out)

    for dy in (0, 1, 3, 2):
        recv(g2_ref.at[0, pl.ds(0, 4 if dy else 3), 0], FALL + dy)
        row = lax.rem(y + NX - dy, NX)
        here = (row // 2, pl.ds(4 * lax.rem(row, 2), 4), c)
        send(g2_ref.at[here], g2_ref.at[here], GFINC, sibling)
        put(g2_ref.at[here], g2_hbm.at[here])
    recv(zred.at[pl.ds(0, NZ - 1), pl.ds(0, 8)], ZALL)
    send(fin_ref.at[c], fin_ref.at[c], FINC, sibling)
    put(fin_ref.at[c], fin_hbm.at[c])
    recv(g2_ref.at[:, :, 0], GFINC)
    put(g2_ref.at[:, :, 1 - c], g2_hbm.at[:, :, 1 - c])
    recv(fin_ref.at[1 - c], FINC)
    put(fin_ref.at[1 - c], fin_hbm.at[1 - c])
    for one in puts:
        one.wait()

    for ref, phase in pending:
        copy(ref, ref, phase, sibling).wait_send()


def lay_out_kernel(
    out_in_ref, b1_in, b2_in, fin_in, g2_in, out_ref, neigh1_ref, self1_ref, bias1_ref, self2_ref, neigh2_ref, bias2_ref
):
    out_ref[...] = out_in_ref[...].astype(bf16)
    neigh1_ref[...] = fin_in[0]
    self1_ref[...] = fin_in[1]
    bias1_ref[...] = b1_in[...]
    bias2_ref[...] = b2_in[...]
    self2_ref[...] = g2_in[0]
    neigh2_ref[...] = g2_in[1]


def body(
    source_feats,
    vertex_feats,
    block_values,
    block_target,
    block_source,
    block_count,
    seed_rows,
    seed_weights,
    neigh_one,
    self_one,
    bias_one,
    self_two,
    neigh_two,
    bias_two,
    output_grad,
):
    vmem = pl.BlockSpec(memory_space=pltpu.VMEM)
    hbm = pl.BlockSpec(memory_space=pl.ANY)
    out_two, bias1, bias2, fin, g2 = pl.pallas_call(
        main_kernel,
        out_shape=(
            jax.ShapeDtypeStruct((2, 256), f32),
            jax.ShapeDtypeStruct((1, 256), f32),
            jax.ShapeDtypeStruct((1, 256), f32),
            jax.ShapeDtypeStruct((2, 64, 256), f32),
            jax.ShapeDtypeStruct((2, 8, 2, 16, 256), f32),
        ),
        in_specs=[hbm] * 13 + [vmem] * 2,
        out_specs=(hbm,) * 5,
        scratch_shapes=[
            pltpu.VMEM((2, 256), f32),
            pltpu.VMEM((2, 1, 256), f32),
            pltpu.VMEM((2, 64, 256), f32),
            pltpu.VMEM((2, 8, 2, 16, 256), f32),
            pltpu.VMEM((1, 64), jnp.int32),
            pltpu.VMEM((1, 64), jnp.int32),
            pltpu.SMEM((1,), jnp.int32),
            pltpu.SMEM((2,), jnp.int32),
            pltpu.VMEM((64, 1024), bf16),
            pltpu.VMEM((64, 128, 128), bf16),
            pltpu.VMEM((32, 64), bf16),
            pltpu.VMEM((64, 256), bf16),
            pltpu.VMEM((64, 256), bf16),
            pltpu.VMEM((1, 256), f32),
            pltpu.VMEM((256, 256), bf16),
            pltpu.VMEM((256, 256), bf16),
            pltpu.VMEM((1, 256), f32),
            pltpu.VMEM((1, 64), jnp.int32),
            pltpu.SMEM((1, 64), jnp.int32),
            pltpu.VMEM((2 * NF, 8, 128), f32),
            pltpu.VMEM((2 * NF, NZ, 4, 128), f32),
            pltpu.VMEM((1024, 256), bf16),
            pltpu.VMEM((2 * NF, 32, 256), f32),
            pltpu.VMEM((1024, 256), bf16),
            pltpu.VMEM((2, 2, NX, 32, 128), f32),
            pltpu.VMEM((2, 32, 256), f32),
            pltpu.VMEM((2, 32, 128), f32),
            pltpu.VMEM((2, NZ, 16, 128), f32),
            pltpu.VMEM((NZ, 16, 128), f32),
            pltpu.VMEM((NZ, 16, 128), f32),
            pltpu.VMEM((2 * NF, 16, 128), f32),
            pltpu.VMEM((NZ, 16, 128), f32),
            pltpu.VMEM((NZ, 16, 128), f32),
            pltpu.VMEM((NZ, 2, 128), f32),
            pltpu.SemaphoreType.DMA((14,)),
            pltpu.SemaphoreType.DMA((10,)),
            pltpu.SemaphoreType.DMA((PHASES,)),
            pltpu.SemaphoreType.DMA((PHASES,)),
        ],
        compiler_params=pltpu.CompilerParams(
            collective_id=1, has_side_effects=True, vmem_limit_bytes=60 * 2**20
        ),
    )(
        block_target.reshape(1, 64),
        block_source.reshape(1, 64),
        block_count,
        seed_rows,
        source_feats,
        block_values,
        vertex_feats.T,
        neigh_one,
        self_one,
        bias_one.reshape(1, 256),
        self_two,
        neigh_two,
        bias_two.reshape(1, 256),
        seed_weights,
        output_grad,
    )
    outs = pl.pallas_call(
        lay_out_kernel,
        out_shape=(
            jax.ShapeDtypeStruct((2, 256), bf16),
            jax.ShapeDtypeStruct((64, 256), f32),
            jax.ShapeDtypeStruct((64, 256), f32),
            jax.ShapeDtypeStruct((1, 256), f32),
            jax.ShapeDtypeStruct((256, 256), f32),
            jax.ShapeDtypeStruct((256, 256), f32),
            jax.ShapeDtypeStruct((1, 256), f32),
        ),
        in_specs=[vmem] * 5,
        out_specs=(vmem,) * 7,
        compiler_params=pltpu.CompilerParams(vmem_limit_bytes=60 * 2**20),
    )(out_two, bias1, bias2, fin, g2.reshape(2, 256, 256))
    out_two, neigh1, self1, bias1, self2, neigh2, bias2 = outs
    return out_two, neigh1, self1, bias1.reshape(256), self2, neigh2, bias2.reshape(256)


def solution(mesh):
    in_specs = (
        P("feat", "graph"),
        P("feat", "graph"),
        P("graph", None, None),
        P("graph"),
        P("graph"),
        P("graph"),
        P(("graph", "feat")),
        P(("graph", "feat"), None),
        P("feat", None),
        P("feat", None),
        P(),
        P(),
        P(),
        P(),
        P(("graph", "feat"), None),
    )
    out_specs = (P(("graph", "feat"), None), P("feat", None), P("feat", None), P(), P(), P(), P())
    return jax.shard_map(body, mesh=mesh, in_specs=in_specs, out_specs=out_specs, check_vma=False)
```
